32 devices in a mesh: groups: 2 (over x), space: 16 (over z, y, core).
Axes of the slice: x: 2, y: 2, z: 4, core: 2. Of those that a mesh axis runs over, the one named last changes fastest.
Arguments:
- grid_inputs: bfloat16 [16384, 474], P(('groups', 'space')), parts along dimension 0, may hold values from -6 to 6
- mesh_latent: bfloat16 [2048, 512], P(('groups', 'space')), parts along dimension 0, may hold values from -6 to 6
- cotangent: bfloat16 [2048, 512], P(('groups', 'space')), parts along dimension 0, may hold values from -6 to 6
- send_list: int32 [32, 16, 8], P(('groups', 'space')), parts along dimension 0, may hold values from 0 to 511
- enc_slot: int32 [2048, 16], P(('groups', 'space')), parts along dimension 0, may hold values from 0 to 639
- enc_mask: int32 [2048, 16], P(('groups', 'space')), parts along dimension 0, may hold values 0 or 1
- halo_list: int32 [32, 2, 64], P(('groups', 'space')), parts along dimension 0, may hold values from 0 to 63
- proc_slot: int32 [2048, 16], P(('groups', 'space')), parts along dimension 0, may hold values from 0 to 191
- proc_mask: int32 [2048, 16], P(('groups', 'space')), parts along dimension 0, may hold values 0 or 1
- w_embed: bfloat16 [474, 512], replicated, may hold values from -0.25 to 0.25
- enc_send: bfloat16 [512, 512], replicated, may hold values from -0.25 to 0.25
- enc_recv: bfloat16 [512, 512], replicated, may hold values from -0.25 to 0.25
- enc_out: bfloat16 [512, 512], replicated, may hold values from -0.25 to 0.25
- proc_send: bfloat16 [512, 512], replicated, may hold values from -0.25 to 0.25
- proc_recv: bfloat16 [512, 512], replicated, may hold values from -0.25 to 0.25
- proc_out: bfloat16 [512, 512], replicated, may hold values from -0.25 to 0.25
Outputs:
- mesh_out: bfloat16 [2048, 512], P(('groups', 'space')), parts along dimension 0
- grad_embed: float32 [948, 512], P('groups'), parts along dimension 0
- grad_enc_send: float32 [1024, 512], P('groups'), parts along dimension 0
- grad_enc_recv: float32 [1024, 512], P('groups'), parts along dimension 0
- grad_enc_out: float32 [1024, 512], P('groups'), parts along dimension 0
- grad_proc_send: float32 [1024, 512], P('groups'), parts along dimension 0
- grad_proc_recv: float32 [1024, 512], P('groups'), parts along dimension 0
- grad_proc_out: float32 [1024, 512], P('groups'), parts along dimension 0
The draws below stay inside these ranges and needn't reach their ends.
There are 2 independent parts, one for each index of `groups`. The reference program is written for one: setup_inputs(seed, part) draws one part's arguments, and reference() takes and returns one part's arrays. A program takes and returns all parts, laid end to end along the dimension named above; an argument that names none is the same for every part. Nothing has to cross between parts.
All inputs are finite; a program needn't handle non-finite values. No bound on the sum of `enc_mask` or of `proc_mask` on one device may be relied on, other than what follows from the above.
Results may differ from the reference program's by a relative error of at most 0.0095.
Values may be sent and summed in bfloat16 or wider, within the bound.
No kernel may reach another device: no remote copies, remote signals or barrier semaphores. Data moves between devices by JAX's collectives and lax.ppermute only.
A program may use at most 128 MiB of HBM per device.

```python
import jax
import jax.numpy as jnp
from jax import lax

L = 512
FIN = 474
G_DEV = 512
M_DEV = 64
F_ENC = 16
F_PROC = 16
CAP = 8
H = 64
G = 8192
M = 1024
N_SPACE = 16


def with_ends(values, own_key, smallest, largest):
    shape = values.shape
    index_at = [jax.random.randint(jax.random.fold_in(own_key, axis), (), 0, shape[axis]) for axis in range(len(shape))]
    values = values.at[tuple(index_at)].set(smallest)
    longest = shape.index(max(shape))
    index_at[longest] = (index_at[longest] + 1) % shape[longest]
    return values.at[tuple(index_at)].set(largest)


def block_levels(rng, dims, shards, smallest, top_value):
    def one(axis_at, blocks):
        draws = jax.random.uniform(jax.random.fold_in(jax.random.fold_in(rng, 6), axis_at), (blocks,), jnp.float32, smallest / len(shards), top_value / len(shards))
        return jnp.repeat(jnp.exp(draws), dims[axis_at] // blocks).reshape((-1,) + (1,) * (len(dims) - axis_at - 1))

    loudness = one(*shards[0])
    for cut in shards[1:]:
        loudness = loudness * one(*cut)
    return loudness


def gaussian(stream_key, dims, spread, reach, split=(), kind=jnp.bfloat16):
    values = jax.random.normal(stream_key, dims, jnp.float32) * spread
    if len(split) > 0:
        values = block_levels(stream_key, dims, split, -0.22, 0.18) * values
    return jnp.clip(values, min=-reach, max=reach).astype(kind)


def setup_inputs(seed: int = 0, part: int = 0) -> dict:
    key_of = jax.random.split(jax.random.key(seed), 17)
    part_keys = jax.random.split(jax.random.fold_in(key_of[16], part), 17)
    grid_inputs = gaussian(part_keys[0], (G, FIN), 1.0, 6.0, ((0, 16),))
    mesh_latent = gaussian(part_keys[1], (M, L), 1.0, 6.0, ((0, 16),))
    cotangent = gaussian(part_keys[2], (M, L), 1.0, 6.0, ((0, 16),))
    send_list = with_ends(jax.random.randint(part_keys[3], (N_SPACE, N_SPACE, CAP), 0, G_DEV), jax.random.fold_in(part_keys[3], 1), 0, G_DEV - 1).astype(jnp.int32)
    enc_slot = with_ends(jax.random.randint(part_keys[4], (M, F_ENC), 0, G_DEV + N_SPACE * CAP), jax.random.fold_in(part_keys[4], 1), 0, (G_DEV + N_SPACE * CAP) - 1).astype(jnp.int32)
    enc_mask = with_ends((jax.random.randint(part_keys[5], (M, F_ENC), 0, 4) < 3).astype(jnp.int32), jax.random.fold_in(part_keys[5], 1), 0, 1)
    halo_list = with_ends(jax.random.randint(part_keys[6], (N_SPACE, 2, H), 0, M_DEV), jax.random.fold_in(part_keys[6], 1), 0, M_DEV - 1).astype(jnp.int32)
    proc_slot = with_ends(jax.random.randint(part_keys[7], (M, F_PROC), 0, M_DEV + 2 * H), jax.random.fold_in(part_keys[7], 1), 0, (M_DEV + 2 * H) - 1).astype(jnp.int32)
    proc_mask = with_ends((jax.random.randint(part_keys[8], (M, F_PROC), 0, 4) < 3).astype(jnp.int32), jax.random.fold_in(part_keys[8], 1), 0, 1)
    w_embed = gaussian(key_of[9], (FIN, L), FIN ** -0.5, 0.25)
    enc_send = gaussian(key_of[10], (L, L), L ** -0.5, 0.25)
    enc_recv = gaussian(key_of[11], (L, L), L ** -0.5, 0.25)
    enc_out = gaussian(key_of[12], (L, L), L ** -0.5, 0.25)
    proc_send = gaussian(key_of[13], (L, L), L ** -0.5, 0.25)
    proc_recv = gaussian(key_of[14], (L, L), L ** -0.5, 0.25)
    proc_out = gaussian(key_of[15], (L, L), L ** -0.5, 0.25)
    return dict(grid_inputs=grid_inputs, mesh_latent=mesh_latent, cotangent=cotangent, send_list=send_list, enc_slot=enc_slot, enc_mask=enc_mask, halo_list=halo_list, proc_slot=proc_slot, proc_mask=proc_mask, w_embed=w_embed, enc_send=enc_send, enc_recv=enc_recv, enc_out=enc_out, proc_send=proc_send, proc_recv=proc_recv, proc_out=proc_out)


def pin(value):
    return value + lax.stop_gradient(value.astype(jnp.bfloat16).astype(jnp.float32) - value)

def mul(left, right):
    return jnp.dot(left, right, precision=lax.Precision.HIGHEST, preferred_element_type=jnp.float32)

def layer_norm(value):
    centred = value - lax.optimization_barrier(jnp.mean(value, axis=-1, keepdims=True))
    return centred * lax.rsqrt(lax.optimization_barrier(jnp.mean(centred * centred, axis=-1, keepdims=True)) + 1e-05)

def embed(inputs, weight):
    return pin(jax.nn.silu(mul(inputs, weight)))

def project(rows, weight):
    return pin(mul(rows, weight))

def node_update(latent, summed, weight):
    return pin(latent + layer_norm(mul(summed, weight)))

def aggregate(table, index, mask, recv_term):
    width = table.shape[1]

    def block_sum(pieces):
        block_index, block_mask, block_recv = pieces
        rows = table[block_index]
        message = jax.nn.silu(rows + block_recv[:, None, :]) * block_mask[..., None].astype(jnp.float32)
        return lax.optimization_barrier(jnp.sum(message, axis=1))
    summed = lax.map(jax.checkpoint(block_sum), (index.reshape(N_SPACE, M_DEV, -1), mask.reshape(N_SPACE, M_DEV, -1), recv_term.reshape(N_SPACE, M_DEV, width)))
    return pin(summed.reshape(-1, width))

def reference(grid_inputs, mesh_latent, cotangent, send_list, enc_slot, enc_mask, halo_list, proc_slot, proc_mask, w_embed, enc_send, enc_recv, enc_out, proc_send, proc_recv, proc_out):
    owner = (jnp.arange(M_DEV * N_SPACE, dtype=jnp.int32) // M_DEV)[:, None]
    offset = jnp.maximum(enc_slot - G_DEV, 0)
    source = offset // CAP
    column = offset % CAP
    remote = send_list[source, owner, column] + source * G_DEV
    enc_index = jnp.where(enc_slot < G_DEV, owner * G_DEV + enc_slot, remote).astype(jnp.int32)
    before = (owner - 1) % N_SPACE
    after = (owner + 1) % N_SPACE
    first = jnp.clip(proc_slot - M_DEV, 0, H - 1)
    second = jnp.clip(proc_slot - M_DEV - H, 0, H - 1)
    from_before = halo_list[before, 1, first] + before * M_DEV
    from_after = halo_list[after, 0, second] + after * M_DEV
    proc_index = jnp.where(proc_slot < M_DEV, owner * M_DEV + proc_slot, jnp.where(proc_slot < M_DEV + H, from_before, from_after)).astype(jnp.int32)
    inputs = grid_inputs.astype(jnp.float32)
    mesh_start = mesh_latent.astype(jnp.float32)

    def forward(w_one, w_two, w_three, w_four, w_five, w_six, w_seven):
        grid = project(embed(inputs, w_one), w_two)
        summed = aggregate(grid, enc_index, enc_mask, mul(mesh_start, w_three))
        middle = node_update(mesh_start, summed, w_four)
        mesh_proj = project(middle, w_five)
        second_sum = aggregate(mesh_proj, proc_index, proc_mask, mul(middle, w_six))
        return node_update(middle, second_sum, w_seven)
    weights = tuple((item.astype(jnp.float32) for item in (w_embed, enc_send, enc_recv, enc_out, proc_send, proc_recv, proc_out)))
    result, pull = jax.vjp(forward, *weights)
    grads = pull(cotangent.astype(jnp.float32))
    return (result.astype(jnp.bfloat16), grads[0], grads[1], grads[2], grads[3], grads[4], grads[5], grads[6])
```

```python
import functools

import jax
import jax.numpy as jnp
from jax import lax
from jax.experimental import pallas as pl
from jax.experimental.pallas import tpu as pltpu
from jax.sharding import PartitionSpec as P

BF = jnp.bfloat16
F32 = jnp.float32
VMEM_BYTES = 40 * 1024 * 1024
BLOCKS = 16


def dot(a, b):
    return lax.dot_general(a, b, (((1,), (0,)), ((), ())), preferred_element_type=F32)


def dot_t(a, b):
    return lax.dot_general(a, b, (((1,), (1,)), ((), ())), preferred_element_type=F32)


def t_dot(a, b):
    return lax.dot_general(a, b, (((0,), (0,)), ((), ())), preferred_element_type=F32)


def sigmoid(v):
    return 0.5 * jnp.tanh(0.5 * v) + 0.5


def silu_slope(v, s):
    return s * (1.0 + v * (1.0 - s))


def normalized(u):
    c = u - jnp.mean(u, axis=-1, keepdims=True)
    r = lax.rsqrt(jnp.mean(c * c, axis=-1, keepdims=True) + 1e-05)
    return c * r, r


def normalized_grad(y, r, g):
    return r * (g - jnp.mean(g, axis=-1, keepdims=True) - y * jnp.mean(g * y, axis=-1, keepdims=True))


def call(body, outs, scratch=(), **kw):
    return pl.pallas_call(
        body,
        out_shape=[jax.ShapeDtypeStruct(s, d) for s, d in outs],
        scratch_shapes=[pltpu.VMEM(s, d) for s, d in scratch],
        compiler_params=pltpu.CompilerParams(vmem_limit_bytes=VMEM_BYTES),
        **kw,
    )


def embed_rows(x, we, ws):
    pre = dot(x, we)
    s = sigmoid(pre)
    lat = (pre * s).astype(BF)
    return lat, silu_slope(pre, s).astype(BF), dot(lat, ws).astype(BF)


def embed_body(x, we, ws, lat, slope, proj):
    lat[...], slope[...], proj[...] = embed_rows(x[...], we[...], ws[...])


def fill_onehot(onehot, slots):
    m, fan = slots.shape
    wide = onehot.shape[1]
    lanes = lax.broadcasted_iota(jnp.int32, (m, wide), 1)
    for f in range(fan):
        onehot[f * m : (f + 1) * m, :] = jnp.where(slots[:, f : f + 1] == lanes, 1.0, 0.0).astype(BF)


def fill_onehot_t(onehot, rows):
    parts, wide = rows.shape
    tall = onehot.shape[0]
    subs = lax.broadcasted_iota(jnp.int32, (tall, wide), 0)
    for p in range(parts):
        onehot[:, p * wide : (p + 1) * wide] = jnp.where(rows[p : p + 1, :] == subs, 1.0, 0.0).astype(BF)


def messages(rows, recv, mask, slope):
    m, fan = mask.shape
    total = None
    for f in range(fan):
        at = slice(f * m, (f + 1) * m)
        v = rows[at, :] + recv
        s = sigmoid(v)
        k = mask[:, f : f + 1].astype(F32)
        slope[at, :] = (silu_slope(v, s) * k).astype(slope.dtype)
        part = v * s * k
        total = part if total is None else total + part
    return total


def encode_body(
    proj, x, we, ws, slots, mask, latent, wrecv, wout, wnext, halo,
    mid, boundary, mesh_proj, agg, y, r, slope, lat_far, slope_far,
    table, onehot, rows,
):
    near = proj.shape[0]
    fill_onehot(onehot, slots)
    table[:near, :] = proj[...]
    lat_far[...], slope_far[...], far = embed_rows(x[...], we[...], ws[...])
    table[near:, :] = far
    rows[...] = dot(onehot[...], table[...])
    recv = dot(latent[...], wrecv[...])
    summed = messages(rows, recv, mask, slope).astype(BF)
    agg[...] = summed
    normed, scale = normalized(dot(summed, wout[...]))
    y[...] = normed
    r[...] = jnp.broadcast_to(scale, r.shape)
    middle = (latent[...].astype(F32) + normed).astype(BF)
    mid[...] = middle
    sent = dot(middle, wnext[...]).astype(BF)
    mesh_proj[...] = sent
    depth = halo.shape[0] // 2
    lanes = lax.broadcasted_iota(jnp.int32, (2 * depth, sent.shape[0]), 1)
    pick = jnp.where(halo[...] == lanes, 1.0, 0.0).astype(BF)
    boundary[...] = dot(pick, sent).astype(BF)


def process_body(
    mesh_proj, left, right, slots, slots_t, mask, mid, wrecv, wout, cotangent,
    out, back, grad_rows, grad_mid, agg, grad_u, grad_recv,
    table, onehot, onehot_t, rows, slope, grad_msg,
):
    m = mesh_proj.shape[0]
    depth = left.shape[0]
    fill_onehot(onehot, slots)
    table[:m, :] = mesh_proj[...]
    table[m : m + depth, :] = left[...]
    table[m + depth : m + 2 * depth, :] = right[...]
    rows[...] = dot(onehot[...], table[...])
    recv = dot(mid[...], wrecv[...])
    summed = messages(rows, recv, mask, slope).astype(BF)
    agg[...] = summed
    normed, scale = normalized(dot(summed, wout[...]))
    out[...] = (mid[...].astype(F32) + normed).astype(BF)
    ct = cotangent[...].astype(F32)
    gu = normalized_grad(normed, scale, ct).astype(BF)
    grad_u[...] = gu
    gagg = dot_t(gu, wout[...])
    gr = message_grads(grad_msg, slope, gagg, mask.shape[1])
    grad_recv[...] = gr
    fill_onehot_t(onehot_t, slots_t)
    grads = dot(onehot_t[...], grad_msg[...])
    grad_rows[...] = grads[:m, :]
    back[...] = grads[m:, :].astype(BF)
    grad_mid[...] = ct + dot_t(gr, wrecv[...])


def message_grads(grad_msg, slope, gagg, fan):
    m = gagg.shape[0]
    total = None
    for f in range(fan):
        at = slice(f * m, (f + 1) * m)
        g = slope[at, :].astype(F32) * gagg
        grad_msg[at, :] = g.astype(BF)
        total = g if total is None else total + g
    return total.astype(BF)


def block_of(place, me, order):
    flips = 0
    for i, step in enumerate(order):
        if place >> (len(order) - 1 - i) & 1:
            flips ^= step
    return me ^ flips


def spread(me, order, grads, keep, send):
    deep = grads[0].shape[0] // BLOCKS
    half = BLOCKS // 2
    for place in range(BLOCKS):
        at = pl.multiple_of(block_of(place, me, order) * deep, deep)
        for g, grad in enumerate(grads):
            rows = grad[pl.ds(at, deep), :]
            to = ((place % half) * len(grads) + g) * deep
            if place < half:
                keep[to : to + deep, :] = rows
            else:
                send[to : to + deep, :] = rows.astype(BF)


def process_grads_body(order, me, agg, grad_u, mid, grad_recv, keep, send, one, two):
    one[...] = t_dot(agg[...], grad_u[...])
    two[...] = t_dot(mid[...], grad_recv[...])
    spread(me[0], order, (one, two), keep, send)


def encode_grads_body(
    order, me, back_left, back_right, halo_t, grad_rows, grad_mid, mid, wnext,
    y, r, agg, wout, slope, slots_t, latent, lat, lat_far, ws, slope_near, slope_far, x, x_far,
    keep, send,
    onehot_t, grad_msg, g_next, g_out, g_recv, g_send, g_embed,
):
    m = mid.shape[0]
    fill_onehot_t(onehot_t, slots_t)
    subs = lax.broadcasted_iota(jnp.int32, (m, halo_t.shape[1]), 0)
    to_left = jnp.where(halo_t[0:1, :] == subs, 1.0, 0.0).astype(BF)
    to_right = jnp.where(halo_t[1:2, :] == subs, 1.0, 0.0).astype(BF)
    gp = (grad_rows[...] + dot(to_right, back_right[...]) + dot(to_left, back_left[...])).astype(BF)
    g_next[...] = t_dot(mid[...], gp)
    gmid = grad_mid[...] + dot_t(gp, wnext[...])
    gu = normalized_grad(y[...], r[:, 0:1], gmid).astype(BF)
    g_out[...] = t_dot(agg[...], gu)
    gagg = dot_t(gu, wout[...])
    gr = message_grads(grad_msg, slope, gagg, grad_msg.shape[0] // m)
    g_recv[...] = t_dot(latent[...], gr)
    gtab = dot(onehot_t[...], grad_msg[...]).astype(BF)
    near = lat.shape[0]
    g_near, g_far = gtab[:near, :], gtab[near:, :]
    g_send[...] = t_dot(lat[...], g_near) + t_dot(lat_far[...], g_far)
    p_near = (dot_t(g_near, ws[...]) * slope_near[...].astype(F32)).astype(BF)
    p_far = (dot_t(g_far, ws[...]) * slope_far[...].astype(F32)).astype(BF)
    fin = x.shape[1]
    tail = fin // 32 * 32
    g_embed[tail:, :] = jnp.zeros((g_embed.shape[0] - tail, g_embed.shape[1]), F32)
    g_embed[:fin, :] = t_dot(x[...], p_near) + t_dot(x_far[...], p_far)
    spread(me[0], order, (g_next, g_out, g_recv, g_send, g_embed), keep, send)


def collect_body(order, counts, *refs):
    me = refs[0][0]
    n_outs = sum(counts)
    ins = refs[1 : 1 + 2 * len(counts)]
    outs = refs[1 + 2 * len(counts) : 1 + 2 * len(counts) + n_outs]
    whole = refs[-1]
    half = BLOCKS // 2
    base = 0
    for i, count in enumerate(counts):
        for place in range(BLOCKS):
            source = ins[2 * i + place // half]
            block = block_of(place, me, order)
            for g in range(count):
                out = outs[base + g]
                short = out.shape[0] != whole.shape[0]
                deep = whole.shape[0] // BLOCKS
                at = pl.multiple_of(block * deep, deep)
                frm = ((place % half) * count + g) * deep
                (whole if short else out)[pl.ds(at, deep), :] = source[frm : frm + deep, :].astype(F32)
        for g in range(count):
            out = outs[base + g]
            if out.shape[0] != whole.shape[0]:
                out[...] = whole[: out.shape[0], :]
        base += count


def exchange(value, step):
    n = lax.axis_size("space")
    return lax.ppermute(value, "space", [(i, i ^ step) for i in range(n)])


def all_sum(keep, send, order, rest):
    for i, step in enumerate(order):
        kept = keep + exchange(send, step).astype(F32)
        if i + 1 < len(order):
            half = kept.shape[0] // 2
            keep, send = kept[:half], kept[half:].astype(BF)
    value = kept.astype(BF)
    for step in rest:
        value = (value.astype(F32) + exchange(value, step).astype(F32)).astype(BF)
    for step in order[:0:-1]:
        value = jnp.concatenate([value, exchange(value, step)], axis=0)
    return value, exchange(value, order[0])


def passed_along(block, distance):
    n = lax.axis_size("space")
    return lax.ppermute(block, "space", [((i - distance) % n, i) for i in range(n)])


SMEM = pl.BlockSpec(memory_space=pltpu.SMEM)
VMEM = pl.BlockSpec(memory_space=pltpu.VMEM)


def local(
    grid_inputs, mesh_latent, cotangent, send_list, enc_slot, enc_mask, halo_list, proc_slot, proc_mask,
    w_embed, enc_send, enc_recv, enc_out, proc_send, proc_recv, proc_out,
):
    n = lax.axis_size("space")
    me = lax.axis_index("space").astype(jnp.int32)
    bits = [1 << i for i in range(n.bit_length() - 1)]
    order, rest = tuple(bits[:4]), tuple(bits[4:])
    mine = (me & (BLOCKS - 1)).reshape(1)
    near, fin = grid_inputs.shape
    m, width = mesh_latent.shape
    edges_e = m * enc_slot.shape[1]
    edges_p = m * proc_slot.shape[1]
    depth = halo_list.shape[2]
    far = send_list.shape[1] * send_list.shape[2]
    enc_rows = enc_slot.T.reshape(-1, 128)
    proc_rows = proc_slot.T.reshape(-1, 128)
    halo = halo_list[0]

    outgoing = grid_inputs[send_list[0]]
    incoming = lax.all_to_all(outgoing, "space", split_axis=0, concat_axis=0, tiled=True)
    x_far = incoming.reshape(far, fin)

    lat, slope_near, proj = call(embed_body, [((near, width), BF)] * 3)(grid_inputs, w_embed, enc_send)

    mid, boundary, mesh_proj, agg, y, r, slope, lat_far, slope_far = call(
        encode_body,
        [((m, width), BF), ((2 * depth, width), BF), ((m, width), BF), ((m, width), BF), ((m, width), F32),
         ((m, 128), F32), ((edges_e, width), BF), ((far, width), BF), ((far, width), BF)],
        [((near + far, width), BF), ((edges_e, near + far), BF), ((edges_e, width), F32)],
    )(proj, x_far, w_embed, enc_send, enc_slot, enc_mask, mesh_latent, enc_recv, enc_out, proc_send,
      halo.reshape(-1, 1))

    from_left = passed_along(boundary[depth:], 1)
    from_right = passed_along(boundary[:depth], -1)

    wide = m + 2 * depth
    out, back, grad_rows, grad_mid, agg2, grad_u, grad_recv = call(
        process_body,
        [((m, width), BF), ((2 * depth, width), BF), ((m, width), F32), ((m, width), F32), ((m, width), BF),
         ((m, width), BF), ((m, width), BF)],
        [((wide, width), BF), ((edges_p, wide), BF), ((wide, edges_p), BF), ((edges_p, width), F32),
         ((edges_p, width), F32), ((edges_p, width), BF)],
    )(mesh_proj, from_left, from_right, proc_slot, proc_rows, proc_mask, mid, proc_recv, proc_out, cotangent)

    back_right = passed_along(back[:depth], -1)
    back_left = passed_along(back[depth:], 1)

    def halves(count):
        rows = count * width // 2
        return [((rows, width), F32), ((rows, width), BF)]

    square = ((width, width), F32)
    keep_p, send_p = call(
        functools.partial(process_grads_body, order), halves(2), [square] * 2, in_specs=[SMEM] + [VMEM] * 4
    )(mine, agg2, grad_u, mid, grad_recv)
    first = all_sum(keep_p, send_p, order, rest)

    keep_e, send_e = call(
        functools.partial(encode_grads_body, order),
        halves(5),
        [((near + far, edges_e), BF), ((edges_e, width), BF)] + [square] * 5,
        in_specs=[SMEM] + [VMEM] * 21,
    )(mine, back_left, back_right, halo, grad_rows, grad_mid, mid, proc_send, y, r, agg, enc_out, slope, enc_rows,
      mesh_latent, lat, lat_far, enc_send, slope_near, slope_far, grid_inputs, x_far)
    second = all_sum(keep_e, send_e, order, rest)

    counts = (2, 5)
    g_pout, g_precv, g_psend, g_eout, g_erecv, g_esend, g_embed = call(
        functools.partial(collect_body, order, counts),
        [square] * 6 + [((fin, width), F32)],
        [square],
        in_specs=[SMEM] + [VMEM] * 4,
    )(mine, *first, *second)
    return out, g_embed, g_esend, g_erecv, g_eout, g_psend, g_precv, g_pout


def solution(mesh):
    rows = P(("groups", "space"), None)
    lists = P(("groups", "space"), None, None)
    return jax.shard_map(
        local,
        mesh=mesh,
        in_specs=(rows, rows, rows, lists, rows, rows, lists, rows, rows) + (P(),) * 7,
        out_specs=(rows,) + (P("groups", None),) * 7,
        check_vma=False,
    )
```

```python
import functools

import jax
import jax.numpy as jnp
from jax import lax
from jax.experimental import pallas as pl
from jax.experimental.pallas import tpu as pltpu
from jax.sharding import PartitionSpec as P

BF = jnp.bfloat16
F32 = jnp.float32
VMEM_BYTES = 16 * 1024 * 1024
BLOCKS = 8


def dot(a, b):
    return lax.dot_general(a, b, (((1,), (0,)), ((), ())), preferred_element_type=F32)


def dot_t(a, b):
    return lax.dot_general(a, b, (((1,), (1,)), ((), ())), preferred_element_type=F32)


def t_dot(a, b):
    return lax.dot_general(a, b, (((0,), (0,)), ((), ())), preferred_element_type=F32)


def sigmoid(v):
    return 0.5 * jnp.tanh(0.5 * v) + 0.5


def silu_slope(v, s):
    return s * (1.0 + v * (1.0 - s))


def normalized(u):
    c = u - jnp.mean(u, axis=-1, keepdims=True)
    r = lax.rsqrt(jnp.mean(c * c, axis=-1, keepdims=True) + 1e-05)
    return c * r, r


def normalized_grad(y, r, g):
    return r * (g - jnp.mean(g, axis=-1, keepdims=True) - y * jnp.mean(g * y, axis=-1, keepdims=True))


class Far:
    def __init__(self, value):
        self.value = pltpu.with_memory_space_constraint(value, pltpu.HBM)
        self.shape, self.dtype = value.shape, value.dtype


class Kept:
    def __init__(self, value):
        self.value = pltpu.with_memory_space_constraint(value, pltpu.HBM)
        self.shape, self.dtype = value.shape, value.dtype


class Input:
    def __init__(self, source, held=None, sem=None):
        self.held, self.copy = source if held is None else held, None
        if held is not None:
            self.copy = pltpu.make_async_copy(source, held, sem)
            self.copy.start()

    def __call__(self):
        if self.copy is not None:
            self.copy.wait()
            self.copy = None
        return self.held


class Output:
    def __init__(self, target, held=None, sem=None):
        self.held, self.copy, self.started = target if held is None else held, None, False
        if held is not None:
            self.copy = pltpu.make_async_copy(held, target, sem)

    def send(self):
        if self.copy is not None:
            self.copy.start()
        self.started = True

    def set(self, value):
        self.held[...] = value.astype(self.held.dtype)
        self.send()


def call(body, name, ins, outs, scratch=(), place=False):
    kept = [v for v in ins if isinstance(v, Kept)]
    far_in = [isinstance(v, (Far, Kept)) for v in ins]
    far_out = [len(v) > 2 for v in outs]
    n_in, n_out, n_kept = len(ins), len(outs), len(kept)

    def kernel(*refs):
        sources, targets = refs[:n_in], refs[n_in : n_in + n_out]
        kept_refs = list(refs[n_in + n_out : n_in + n_out + n_kept])
        rest = list(refs[n_in + n_out + n_kept :])
        out_sems, in_sems = rest.pop(), rest.pop()
        inputs, outputs = [], []
        for i, v in enumerate(ins):
            if isinstance(v, Kept):
                inputs.append(Input(sources[i], kept_refs.pop(0), in_sems.at[i]))
            elif isinstance(v, Far):
                inputs.append(Input(sources[i], rest.pop(0), in_sems.at[i]))
            else:
                inputs.append(Input(sources[i]))
        for i, is_far in enumerate(far_out):
            outputs.append(Output(targets[i], rest.pop(0), out_sems.at[i]) if is_far else Output(targets[i]))
        lead = (lax.axis_index("space").astype(jnp.int32) & (BLOCKS - 1),) if place else ()
        body(*lead, inputs, outputs, rest)
        for value in inputs:
            value()
        for value in outputs:
            if not value.started:
                value.send()
        for value in outputs:
            if value.copy is not None:
                value.copy.wait()

    anywhere, near = pl.BlockSpec(memory_space=pl.ANY), pl.BlockSpec(memory_space=pltpu.VMEM)
    held = [pltpu.VMEM(v.shape, v.dtype) for v in ins if isinstance(v, Far)]
    held += [pltpu.VMEM(v[0], v[1]) for v in outs if len(v) > 2]
    return pl.pallas_call(
        kernel,
        name=name,
        out_shape=[(pltpu.HBM if far else pltpu.VMEM)(v[0], v[1]) for v, far in zip(outs, far_out)]
        + [pltpu.VMEM(v.shape, v.dtype) for v in kept],
        in_specs=[anywhere if far else near for far in far_in],
        out_specs=[anywhere if far else near for far in far_out] + [near] * n_kept,
        scratch_shapes=held
        + [pltpu.VMEM(shape, dtype) for shape, dtype in scratch]
        + [pltpu.SemaphoreType.DMA((n_in,)), pltpu.SemaphoreType.DMA((max(n_out, 1),))],
        compiler_params=pltpu.CompilerParams(vmem_limit_bytes=VMEM_BYTES),
    )(*(v.value if far else v for v, far in zip(ins, far_in)))


def pick_body(ins, outs, _):
    sends_t, x_t = ins
    sends = sends_t()[...]
    cap, peers = sends.shape
    lanes = lax.broadcasted_iota(jnp.int32, (cap, x_t.held.shape[1]), 1)
    pick = [jnp.where(sends[:, d : d + 1] == lanes, 1.0, 0.0) for d in range(peers)]
    pick = jnp.concatenate(pick, axis=0).astype(BF)
    outs[0].set(dot_t(pick, x_t()[...]))


def embed_rows(pre, ws):
    s = sigmoid(pre)
    lat = (pre * s).astype(BF)
    return lat, silu_slope(pre, s).astype(BF), dot(lat, ws).astype(BF)


def embed_body(ins, outs, _):
    x_t, we, ws, latent, wrecv = ins[:5]
    lat, slope, proj, recv = outs
    x_t()
    at = t_dot(x_t()[...], we()[...])
    one, two, three = embed_rows(at, ws()[...])
    lat.set(one)
    slope.set(two)
    proj.set(three)
    recv.set(dot(latent()[...], wrecv()[...]))


def fill_onehot(onehot, slots):
    m, fan = slots.shape
    wide = onehot.shape[1]
    lanes = lax.broadcasted_iota(jnp.int32, (m, wide), 1)
    for f in range(fan):
        onehot[f * m : (f + 1) * m, :] = jnp.where(slots[:, f : f + 1] == lanes, 1.0, 0.0).astype(BF)


def fill_onehot_t(onehot, slots_t):
    fan, m = slots_t.shape
    tall = onehot.shape[0]
    subs = lax.broadcasted_iota(jnp.int32, (tall, 2 * m), 0)
    for f in range(0, fan, 2):
        pair = jnp.concatenate([slots_t[f : f + 1, :], slots_t[f + 1 : f + 2, :]], axis=1)
        onehot[:, f * m : (f + 2) * m] = jnp.where(pair == subs, 1.0, 0.0).astype(BF)


def messages(rows, recv, mask, slope):
    m, fan = mask.shape
    total = None
    for f in range(fan):
        at = slice(f * m, (f + 1) * m)
        v = rows[at, :] + recv
        s = sigmoid(v)
        k = mask[:, f : f + 1].astype(F32)
        slope[at, :] = (silu_slope(v, s) * k).astype(slope.dtype)
        part = v * s * k
        total = part if total is None else total + part
    return total.astype(BF)


def encode_body(ins, outs, scratch):
    slots_t, mask_t, x, we, ws, proj, recv, wout, latent, wnext, halo = ins
    mid, to_left, to_right, mesh_proj, agg, y, r, slope, lat_far, slope_far = outs
    table, onehot, rows = scratch
    near = proj.held.shape[0]
    fill_onehot(onehot, slots_t()[...].T)
    mask = mask_t()[...].T
    x()
    pre = dot(x()[...], we()[...])
    one, two, far = embed_rows(pre, ws()[...])
    lat_far.set(one)
    slope_far.set(two)
    table[near:, :] = far
    table[:near, :] = proj()[...]
    rows[...] = dot(onehot[...], table[...])
    summed = messages(rows, recv()[...], mask, slope.held)
    slope.send()
    agg.set(summed)
    normed, scale = normalized(dot(summed, wout()[...]))
    y.set(normed)
    r.set(jnp.broadcast_to(scale, r.held.shape))
    middle = (latent()[...].astype(F32) + normed).astype(BF)
    mid.set(middle)
    sent = dot(middle, wnext()[...]).astype(BF)
    mesh_proj.set(sent)
    lists = halo()[...]
    subs = lax.broadcasted_iota(jnp.int32, (sent.shape[0], lists.shape[1]), 0)
    to_left.set(t_dot(jnp.where(lists[0:1, :] == subs, 1.0, 0.0).astype(BF), sent))
    to_right.set(t_dot(jnp.where(lists[1:2, :] == subs, 1.0, 0.0).astype(BF), sent))


def process_body(ins, outs, scratch):
    slots_t, mask_t, mesh_proj, left, right, mid, wrecv, wout, cotangent = ins
    out, to_left, to_right, grad_rows, grad_mid, agg, grad_u, grad_recv = outs
    table, onehot, onehot_t, rows, slope, grad_msg = scratch
    m = mesh_proj.held.shape[0]
    depth = left.held.shape[0]
    slots = slots_t()[...]
    fill_onehot(onehot, slots.T)
    mask = mask_t()[...].T
    fill_onehot_t(onehot_t, slots)
    table[:m, :] = mesh_proj()[...]
    table[m : m + depth, :] = left()[...]
    table[m + depth : m + 2 * depth, :] = right()[...]
    rows[...] = dot(onehot[...], table[...])
    middle = mid()[...]
    summed = messages(rows, dot(middle, wrecv()[...]), mask, slope)
    agg.set(summed)
    normed, scale = normalized(dot(summed, wout()[...]))
    out.set(middle.astype(F32) + normed)
    ct = cotangent()[...].astype(F32)
    gu = normalized_grad(normed, scale, ct).astype(BF)
    grad_u.set(gu)
    gr = message_grads(grad_msg, slope, dot_t(gu, wout()[...]), mask.shape[1])
    grad_recv.set(gr)
    grads = dot(onehot_t[...], grad_msg[...])
    to_left.set(grads[m : m + depth, :])
    to_right.set(grads[m + depth :, :])
    grad_rows.set(grads[:m, :])
    grad_mid.set(ct + dot_t(gr, wrecv()[...]))


def message_grads(grad_msg, slope, gagg, fan):
    m = gagg.shape[0]
    total = None
    for f in range(fan):
        at = slice(f * m, (f + 1) * m)
        g = slope[at, :].astype(F32) * gagg
        grad_msg[at, :] = g.astype(BF)
        total = g if total is None else total + g
    return total.astype(BF)


def block_of(place, me, order):
    flips = 0
    for i, step in enumerate(order):
        if place >> (len(order) - 1 - i) & 1:
            flips ^= step
    return me ^ flips


def spread(me, order, grads, keep, send):
    deep = grads[0].shape[0] // BLOCKS
    half = BLOCKS // 2
    for place in reversed(range(BLOCKS)):
        at = pl.multiple_of(block_of(place, me, order) * deep, deep)
        for g, grad in enumerate(grads):
            to = ((place % half) * len(grads) + g) * deep
            target = keep if place < half else send
            target.held[to : to + deep, :] = grad[pl.ds(at, deep), :].astype(target.held.dtype)
        if place == half:
            send.send()
    keep.send()


def process_grads_body(order, me, ins, outs, scratch):
    agg, grad_u, mid, grad_recv = ins
    one, two = scratch
    one[...] = t_dot(agg()[...], grad_u()[...])
    two[...] = t_dot(mid()[...], grad_recv()[...])
    spread(me, order, (one, two), *outs)


def mesh_grads_body(order, me, ins, outs, scratch):
    slots_t, back_left, back_right, halo, grad_rows, wnext, grad_mid, y, r, wout, slope, mid, agg, latent = ins
    keep, send, grad_table = outs
    onehot_t, grad_msg, g_next, g_out, g_recv = scratch
    m = mid.held.shape[0]
    fill_onehot_t(onehot_t, slots_t()[...])
    lists = halo()[...]
    subs = lax.broadcasted_iota(jnp.int32, (m, lists.shape[1]), 0)
    to_left = jnp.where(lists[0:1, :] == subs, 1.0, 0.0).astype(BF)
    to_right = jnp.where(lists[1:2, :] == subs, 1.0, 0.0).astype(BF)
    gp = (grad_rows()[...] + dot(to_right, back_right()[...]) + dot(to_left, back_left()[...])).astype(BF)
    gmid = grad_mid()[...] + dot_t(gp, wnext()[...])
    gu = normalized_grad(y()[...], r()[:, 0:1], gmid).astype(BF)
    gagg = dot_t(gu, wout()[...])
    gr = message_grads(grad_msg, slope(), gagg, grad_msg.shape[0] // m)
    grad_table.set(dot(onehot_t[...], grad_msg[...]))
    g_next[...] = t_dot(mid()[...], gp)
    g_out[...] = t_dot(agg()[...], gu)
    g_recv[...] = t_dot(latent()[...], gr)
    spread(me, order, (g_next, g_out, g_recv), keep, send)


def grid_grads_body(order, me, ins, outs, scratch):
    grad_table, ws, slope_near, slope_far, x_t, x_far, lat, lat_far = ins
    g_send, g_embed = scratch
    near = lat.held.shape[0]
    g_near, g_far = grad_table()[:near, :], grad_table()[near:, :]
    p_near = (dot_t(g_near, ws()[...]) * slope_near()[...].astype(F32)).astype(BF)
    p_far = (dot_t(g_far, ws()[...]) * slope_far()[...].astype(F32)).astype(BF)
    fin = x_t.held.shape[0]
    tail = fin // 32 * 32
    g_embed[tail:, :] = jnp.zeros((g_embed.shape[0] - tail, g_embed.shape[1]), F32)
    g_embed[:fin, :] = dot(x_t()[...], p_near) + t_dot(x_far()[...], p_far)
    g_send[...] = t_dot(lat()[...], g_near) + t_dot(lat_far()[...], g_far)
    spread(me, order, (g_send, g_embed), *outs)


def collect_body(order, me, ins, outs, scratch):
    whole = scratch[0] if scratch else outs[0].held
    half = BLOCKS // 2
    deep = whole.shape[0] // BLOCKS
    for g, out in enumerate(outs):
        short = out.held.shape[0] != whole.shape[0]
        for place in range(BLOCKS):
            source = ins[place // half]()
            at = pl.multiple_of(block_of(place, me, order) * deep, deep)
            frm = ((place % half) * len(outs) + g) * deep
            (whole if short else out.held)[pl.ds(at, deep), :] = source[frm : frm + deep, :].astype(F32)
        if short:
            out.held[...] = whole[: out.held.shape[0], :]
        out.send()


def add_body(ins, outs, _):
    kept, got = ins
    total = kept()[...].astype(F32) + got()[...].astype(F32)
    deep = 0
    for out in outs:
        out.set(total[deep : deep + out.held.shape[0], :])
        deep += out.held.shape[0]


def join_body(ins, outs, _):
    half = ins[0].held.shape[0]
    outs[0].held[:half, :] = ins[0]()[...]
    outs[0].held[half:, :] = ins[1]()[...]


def load_body(ins, outs, _):
    for value in ins:
        value()


def exchange(value, step):
    n = lax.axis_size("space")
    return lax.ppermute(value, "space", [(i, i ^ step) for i in range(n)])


def all_sum(name, keep, send, order, rest):
    for i, step in enumerate(order):
        rows, width = keep.shape
        if i + 1 < len(order):
            outs = [((rows // 2, width), F32), ((rows // 2, width), BF)]
        else:
            outs = [((rows, width), BF)]
        got = call(add_body, f"{name}_add", [keep, exchange(send, step)], outs)
        if i + 1 < len(order):
            keep, send = got
    (value,) = got
    for step in rest:
        (value,) = call(add_body, f"{name}_add", [value, exchange(value, step)], [(value.shape, BF)])
    for step in order[:0:-1]:
        rows, width = value.shape
        (value,) = call(join_body, f"{name}_join", [value, exchange(value, step)], [((2 * rows, width), BF)])
    return value, exchange(value, order[0])


def passed_along(block, distance):
    n = lax.axis_size("space")
    return lax.ppermute(block, "space", [((i - distance) % n, i) for i in range(n)])


def local(
    grid_inputs, mesh_latent, cotangent, send_list, enc_slot, enc_mask, halo_list, proc_slot, proc_mask,
    w_embed, enc_send, enc_recv, enc_out, proc_send, proc_recv, proc_out,
):
    n = lax.axis_size("space")
    bits = [1 << i for i in range(n.bit_length() - 1)]
    y_first = tuple(bits[:3])
    z_first = (bits[0], bits[2], bits[1])
    rest = tuple(bits[3:])
    near, fin = grid_inputs.shape
    m, width = mesh_latent.shape
    edges_e = m * enc_slot.shape[1]
    edges_p = m * proc_slot.shape[1]
    depth = halo_list.shape[2]
    far = send_list.shape[1] * send_list.shape[2]
    x_t, sends_t, enc_slot_t, enc_mask_t, proc_slot_t, proc_mask_t = (
        v.T for v in (grid_inputs, send_list[0], enc_slot, enc_mask, proc_slot, proc_mask)
    )
    halo = halo_list[0]

    (outgoing,) = call(pick_body, "pick", [Far(sends_t), Far(x_t)], [((far, fin), BF, "far")])
    incoming = lax.all_to_all(outgoing.reshape(n, -1, fin), "space", split_axis=0, concat_axis=0, tiled=True)
    x_far = incoming.reshape(far, fin)

    patch, edge_rows, patch_f32 = ((m, width), BF), ((depth, width), BF), ((m, width), F32)
    grid_rows, far_rows = ((near, width), BF), ((far, width), BF)
    lat, slope_near, proj, recv, w_embed, enc_send, latent, enc_out, proc_send, halo, enc_slot_t, enc_mask_t = call(
        embed_body,
        "embed",
        [Far(x_t), Kept(w_embed), Kept(enc_send), Kept(mesh_latent), Far(enc_recv), Kept(enc_out), Kept(proc_send),
         Kept(halo), Kept(enc_slot_t), Kept(enc_mask_t)],
        [(*grid_rows, "far"), (*grid_rows, "far"), grid_rows, patch_f32],
    )

    mid, to_left, to_right, mesh_proj, agg, y, r, slope, lat_far, slope_far = call(
        encode_body,
        "encode",
        [enc_slot_t, enc_mask_t, x_far, w_embed, enc_send, proj, recv, enc_out, latent, proc_send, halo],
        [patch, edge_rows, edge_rows, patch, patch, patch_f32, ((m, 128), F32), ((edges_e, width), BF), far_rows,
         far_rows],
        [((near + far, width), BF), ((edges_e, near + far), BF), ((edges_e, width), F32)],
    )

    from_left = passed_along(to_right, 1)
    from_right = passed_along(to_left, -1)

    after = (x_t, lat, slope_near, proc_recv, proc_out, cotangent, proc_slot_t, proc_mask_t, mid)
    x_t, lat, slope_near, proc_recv, proc_out, cotangent, proc_slot_t, proc_mask_t, mid = lax.optimization_barrier(after)
    x_t, lat, slope_near, proc_recv, proc_out, cotangent, proc_slot_t, proc_mask_t = call(
        load_body,
        "load",
        [Kept(v) for v in (x_t, lat, slope_near, proc_recv, proc_out, cotangent, proc_slot_t, proc_mask_t)],
        [],
    )

    wide = m + 2 * depth
    out, back_to_left, back_to_right, grad_rows, grad_mid, agg2, grad_u, grad_recv = call(
        process_body,
        "process",
        [proc_slot_t, proc_mask_t, mesh_proj, from_left, from_right, mid, proc_recv, proc_out, cotangent],
        [(*patch, "far"), edge_rows, edge_rows, patch_f32, patch_f32, patch, patch, patch],
        [((wide, width), BF), ((edges_p, wide), BF), ((wide, edges_p), BF), ((edges_p, width), F32),
         ((edges_p, width), F32), ((edges_p, width), BF)],
    )

    back_right = passed_along(back_to_left, -1)
    back_left = passed_along(back_to_right, 1)

    def halves(count):
        rows = count * width // 2
        return [((rows, width), F32), ((rows, width), BF)]

    square = ((width, width), F32)

    def collected(name, order, pair, outs, scratch=()):
        outs = [(*v, "far") for v in outs]
        return call(functools.partial(collect_body, order), name, pair, outs, scratch, True)

    keep_p, send_p = call(
        functools.partial(process_grads_body, z_first), "process_grads", [agg2, grad_u, mid, grad_recv], halves(2),
        [square] * 2, True,
    )
    grad_rows, keep_p, send_p = lax.optimization_barrier((grad_rows, keep_p, send_p))
    first = all_sum("process", keep_p, send_p, z_first, rest)

    keep_m, send_m, grad_table = call(
        functools.partial(mesh_grads_body, y_first),
        "mesh_grads",
        [enc_slot_t, back_left, back_right, halo, grad_rows, proc_send, grad_mid, y, r, enc_out, slope, mid, agg,
         latent],
        halves(3) + [((near + far, width), BF)],
        [((near + far, edges_e), BF), ((edges_e, width), BF)] + [square] * 3,
        True,
    )
    second = all_sum("mesh", keep_m, send_m, y_first, rest)

    keep_g, send_g = call(
        functools.partial(grid_grads_body, z_first),
        "grid_grads",
        [grad_table, enc_send, slope_near, slope_far, x_t, x_far, lat, lat_far],
        halves(2),
        [square] * 2,
        True,
    )
    third = all_sum("grid", keep_g, send_g, z_first, rest)

    g_pout, g_precv = collected("collect_process", z_first, first, [square] * 2)
    g_psend, g_eout, g_erecv = collected("collect_mesh", y_first, second, [square] * 3)
    g_esend, g_embed = collected("collect_grid", z_first, third, [square, ((fin, width), F32)], [square])
    return out, g_embed, g_esend, g_erecv, g_eout, g_psend, g_precv, g_pout


def solution(mesh):
    rows = P(("groups", "space"), None)
    lists = P(("groups", "space"), None, None)
    return jax.shard_map(
        local,
        mesh=mesh,
        in_specs=(rows, rows, rows, lists, rows, rows, lists, rows, rows) + (P(),) * 7,
        out_specs=(rows,) + (P("groups", None),) * 7,
        check_vma=False,
    )
```

```python
import functools

import jax
import jax.numpy as jnp
from jax import lax
from jax.experimental import pallas as pl
from jax.experimental.pallas import tpu as pltpu
from jax.sharding import PartitionSpec as P

BF = jnp.bfloat16
F32 = jnp.float32
VMEM_BYTES = 16 * 1024 * 1024
BLOCKS = 8
ORDER_P, ORDER_M, ORDER_G = (1, 2, 4), (1, 2, 4), (1, 4, 2)
PLAN = "p2 mesh1 m2 grid2 p2 g2 m2 g2 p2 m2 p2 g2 p2 m2 g2 p2 m2 g2 p2 m2 g2 p2 g2 m2 g2 m2"
WEIGHTS = (1, 10**9, 10**10, 10**11)
FIRST = (0, 0, 0, 0, 0, 0)


def dot(a, b):
    return lax.dot_general(a, b, (((1,), (0,)), ((), ())), preferred_element_type=F32)


def dot_t(a, b):
    return lax.dot_general(a, b, (((1,), (1,)), ((), ())), preferred_element_type=F32)


def t_dot(a, b):
    return lax.dot_general(a, b, (((0,), (0,)), ((), ())), preferred_element_type=F32)


def sigmoid(v):
    return 0.5 * jnp.tanh(0.5 * v) + 0.5


def silu_slope(v, s):
    return s * (1.0 + v * (1.0 - s))


def normalized(u):
    c = u - jnp.mean(u, axis=-1, keepdims=True)
    r = lax.rsqrt(jnp.mean(c * c, axis=-1, keepdims=True) + 1e-05)
    return c * r, r


def normalized_grad(y, r, g):
    return r * (g - jnp.mean(g, axis=-1, keepdims=True) - y * jnp.mean(g * y, axis=-1, keepdims=True))


class Far:
    def __init__(self, value):
        self.value = pltpu.with_memory_space_constraint(value, pltpu.HBM)
        self.shape, self.dtype = value.shape, value.dtype


class Kept:
    def __init__(self, value):
        self.value = pltpu.with_memory_space_constraint(value, pltpu.HBM)
        self.shape, self.dtype = value.shape, value.dtype


class Input:
    def __init__(self, source, held=None, sem=None):
        self.held, self.copy = source if held is None else held, None
        if held is not None:
            self.copy = pltpu.make_async_copy(source, held, sem)
            self.copy.start()

    def __call__(self):
        if self.copy is not None:
            self.copy.wait()
            self.copy = None
        return self.held


class Output:
    def __init__(self, target, held=None, sem=None):
        self.held, self.copy, self.started = target if held is None else held, None, False
        if held is not None:
            self.copy = pltpu.make_async_copy(held, target, sem)

    def send(self):
        if self.copy is not None:
            self.copy.start()
        self.started = True

    def set(self, value):
        self.held[...] = value.astype(self.held.dtype)
        self.send()


def call(body, name, ins, outs, scratch=(), place=False, after=None, weight=0):
    kept = [v for v in ins if isinstance(v, Kept)]
    far_in = [isinstance(v, (Far, Kept)) for v in ins]
    far_out = [len(v) > 2 for v in outs]
    n_in, n_out, n_kept = len(ins), len(outs), len(kept)
    lead = () if after is None else (after,)

    def kernel(*refs):
        refs = refs[len(lead) :]
        sources, targets = refs[:n_in], refs[n_in : n_in + n_out]
        kept_refs = list(refs[n_in + n_out : n_in + n_out + n_kept])
        rest = list(refs[n_in + n_out + n_kept :])
        out_sems, in_sems = rest.pop(), rest.pop()
        inputs, outputs = [], []
        for i, v in enumerate(ins):
            if isinstance(v, Kept):
                inputs.append(Input(sources[i], kept_refs.pop(0), in_sems.at[i]))
            elif isinstance(v, Far):
                inputs.append(Input(sources[i], rest.pop(0), in_sems.at[i]))
            else:
                inputs.append(Input(sources[i]))
        for i, is_far in enumerate(far_out):
            outputs.append(Output(targets[i], rest.pop(0), out_sems.at[i]) if is_far else Output(targets[i]))
        where = (lax.axis_index("space").astype(jnp.int32) & (BLOCKS - 1),) if place else ()
        body(*where, inputs, outputs, rest)
        for value in inputs:
            value()
        for value in outputs:
            if not value.started:
                value.send()
        for value in outputs:
            if value.copy is not None:
                value.copy.wait()

    anywhere, near = pl.BlockSpec(memory_space=pl.ANY), pl.BlockSpec(memory_space=pltpu.VMEM)
    held = [pltpu.VMEM(v.shape, v.dtype) for v in ins if isinstance(v, Far)]
    held += [pltpu.VMEM(v[0], v[1]) for v in outs if len(v) > 2]
    return pl.pallas_call(
        kernel,
        name=name,
        out_shape=[(pltpu.HBM if far else pltpu.VMEM)(v[0], v[1]) for v, far in zip(outs, far_out)]
        + [pltpu.VMEM(v.shape, v.dtype) for v in kept],
        in_specs=[anywhere] * len(lead) + [anywhere if far else near for far in far_in],
        out_specs=[anywhere if far else near for far in far_out] + [near] * n_kept,
        scratch_shapes=held
        + [pltpu.VMEM(shape, dtype) for shape, dtype in scratch]
        + [pltpu.SemaphoreType.DMA((n_in,)), pltpu.SemaphoreType.DMA((max(n_out, 1),))],
        compiler_params=pltpu.CompilerParams(vmem_limit_bytes=VMEM_BYTES),
        cost_estimate=pl.CostEstimate(flops=WEIGHTS[weight], bytes_accessed=1, transcendentals=0),
    )(*lead, *(v.value if far else v for v, far in zip(ins, far_in)))


def pick_body(ins, outs, _):
    sends_t, x_t = ins
    sends = sends_t()[...]
    cap, peers = sends.shape
    lanes = lax.broadcasted_iota(jnp.int32, (cap, x_t.held.shape[1]), 1)
    pick = [jnp.where(sends[:, d : d + 1] == lanes, 1.0, 0.0) for d in range(peers)]
    pick = jnp.concatenate(pick, axis=0).astype(BF)
    outs[0].set(dot_t(pick, x_t()[...]))


def embed_rows(pre, ws):
    s = sigmoid(pre)
    lat = (pre * s).astype(BF)
    return lat, silu_slope(pre, s).astype(BF), dot(lat, ws).astype(BF)


def embed_body(ins, outs, _):
    x_t, we, ws, latent, wrecv = ins[:5]
    lat, slope, proj, recv = outs
    x_t()
    at = t_dot(x_t()[...], we()[...])
    one, two, three = embed_rows(at, ws()[...])
    lat.set(one)
    slope.set(two)
    proj.set(three)
    recv.set(dot(latent()[...], wrecv()[...]))


def fill_onehot(onehot, slots):
    m, fan = slots.shape
    wide = onehot.shape[1]
    lanes = lax.broadcasted_iota(jnp.int32, (m, wide), 1)
    for f in range(fan):
        onehot[f * m : (f + 1) * m, :] = jnp.where(slots[:, f : f + 1] == lanes, 1.0, 0.0).astype(BF)


def fill_onehot_t(onehot, slots_t):
    fan, m = slots_t.shape
    tall = onehot.shape[0]
    subs = lax.broadcasted_iota(jnp.int32, (tall, 2 * m), 0)
    for f in range(0, fan, 2):
        pair = jnp.concatenate([slots_t[f : f + 1, :], slots_t[f + 1 : f + 2, :]], axis=1)
        onehot[:, f * m : (f + 2) * m] = jnp.where(pair == subs, 1.0, 0.0).astype(BF)


def messages(rows, recv, mask, slope):
    m, fan = mask.shape
    total = None
    for f in range(fan):
        at = slice(f * m, (f + 1) * m)
        v = rows[at, :] + recv
        s = sigmoid(v)
        k = mask[:, f : f + 1].astype(F32)
        slope[at, :] = (silu_slope(v, s) * k).astype(slope.dtype)
        part = v * s * k
        total = part if total is None else total + part
    return total.astype(BF)


def encode_body(ins, outs, scratch):
    slots_t, mask_t, x, we, ws, proj, recv, wout, latent, wnext, halo = ins
    mid, to_left, to_right, mesh_proj, agg, y, r, slope, lat_far, slope_far = outs
    table, onehot, rows = scratch
    near = proj.held.shape[0]
    fill_onehot(onehot, slots_t()[...].T)
    mask = mask_t()[...].T
    x()
    pre = dot(x()[...], we()[...])
    one, two, far = embed_rows(pre, ws()[...])
    lat_far.set(one)
    slope_far.set(two)
    table[near:, :] = far
    table[:near, :] = proj()[...]
    rows[...] = dot(onehot[...], table[...])
    summed = messages(rows, recv()[...], mask, slope.held)
    slope.send()
    agg.set(summed)
    normed, scale = normalized(dot(summed, wout()[...]))
    y.set(normed)
    r.set(jnp.broadcast_to(scale, r.held.shape))
    middle = (latent()[...].astype(F32) + normed).astype(BF)
    mid.set(middle)
    sent = dot(middle, wnext()[...]).astype(BF)
    mesh_proj.set(sent)
    lists = halo()[...]
    subs = lax.broadcasted_iota(jnp.int32, (sent.shape[0], lists.shape[1]), 0)
    to_left.set(t_dot(jnp.where(lists[0:1, :] == subs, 1.0, 0.0).astype(BF), sent))
    to_right.set(t_dot(jnp.where(lists[1:2, :] == subs, 1.0, 0.0).astype(BF), sent))


def process_body(ins, outs, scratch):
    slots_t, mask_t, mesh_proj, left, right, mid, wrecv, wout, cotangent = ins
    out, to_left, to_right, grad_rows, grad_mid, agg, grad_u, grad_recv = outs
    table, onehot, onehot_t, rows, slope, grad_msg = scratch
    m = mesh_proj.held.shape[0]
    depth = left.held.shape[0]
    slots = slots_t()[...]
    fill_onehot(onehot, slots.T)
    mask = mask_t()[...].T
    fill_onehot_t(onehot_t, slots)
    table[:m, :] = mesh_proj()[...]
    table[m : m + depth, :] = left()[...]
    table[m + depth : m + 2 * depth, :] = right()[...]
    rows[...] = dot(onehot[...], table[...])
    middle = mid()[...]
    summed = messages(rows, dot(middle, wrecv()[...]), mask, slope)
    agg.set(summed)
    normed, scale = normalized(dot(summed, wout()[...]))
    out.set(middle.astype(F32) + normed)
    ct = cotangent()[...].astype(F32)
    gu = normalized_grad(normed, scale, ct).astype(BF)
    grad_u.set(gu)
    gr = message_grads(grad_msg, slope, dot_t(gu, wout()[...]), mask.shape[1])
    grad_recv.set(gr)
    grads = dot(onehot_t[...], grad_msg[...])
    to_left.set(grads[m : m + depth, :])
    to_right.set(grads[m + depth :, :])
    grad_rows.set(grads[:m, :])
    grad_mid.set(ct + dot_t(gr, wrecv()[...]))


def message_grads(grad_msg, slope, gagg, fan):
    m = gagg.shape[0]
    total = None
    for f in range(fan):
        at = slice(f * m, (f + 1) * m)
        g = slope[at, :].astype(F32) * gagg
        grad_msg[at, :] = g.astype(BF)
        total = g if total is None else total + g
    return total.astype(BF)


def block_of(place, me, order):
    flips = 0
    for i, step in enumerate(order):
        if place >> (len(order) - 1 - i) & 1:
            flips ^= step
    return me ^ flips


def spread(me, order, grads, keep, send):
    deep = grads[0].shape[0] // BLOCKS
    half = BLOCKS // 2
    for place in reversed(range(BLOCKS)):
        at = pl.multiple_of(block_of(place, me, order) * deep, deep)
        for g, grad in enumerate(grads):
            to = ((place % half) * len(grads) + g) * deep
            target = keep if place < half else send
            target.held[to : to + deep, :] = grad[pl.ds(at, deep), :].astype(target.held.dtype)
        if place == half:
            send.send()
    keep.send()


def process_grads_body(order, me, ins, outs, scratch):
    agg, grad_u, mid, grad_recv = ins
    one, two = scratch
    one[...] = t_dot(agg()[...], grad_u()[...])
    two[...] = t_dot(mid()[...], grad_recv()[...])
    spread(me, order, (one, two), *outs)


def mesh_grads_body(order, me, ins, outs, scratch):
    slots_t, back_left, back_right, halo, grad_rows, wnext, grad_mid, y, r, wout, slope, mid, agg, latent = ins
    keep, send, grad_table = outs
    onehot_t, grad_msg, g_next, g_out, g_recv = scratch
    m = mid.held.shape[0]
    fill_onehot_t(onehot_t, slots_t()[...])
    lists = halo()[...]
    subs = lax.broadcasted_iota(jnp.int32, (m, lists.shape[1]), 0)
    to_left = jnp.where(lists[0:1, :] == subs, 1.0, 0.0).astype(BF)
    to_right = jnp.where(lists[1:2, :] == subs, 1.0, 0.0).astype(BF)
    gp = (grad_rows()[...] + dot(to_right, back_right()[...]) + dot(to_left, back_left()[...])).astype(BF)
    gmid = grad_mid()[...] + dot_t(gp, wnext()[...])
    gu = normalized_grad(y()[...], r()[:, 0:1], gmid).astype(BF)
    gagg = dot_t(gu, wout()[...])
    gr = message_grads(grad_msg, slope(), gagg, grad_msg.shape[0] // m)
    grad_table.set(dot(onehot_t[...], grad_msg[...]))
    g_next[...] = t_dot(mid()[...], gp)
    g_out[...] = t_dot(agg()[...], gu)
    g_recv[...] = t_dot(latent()[...], gr)
    spread(me, order, (g_next, g_out, g_recv), keep, send)


def grid_grads_body(order, me, ins, outs, scratch):
    grad_table, ws, slope_near, slope_far, x_t, x_far, lat, lat_far = ins
    g_send, g_embed = scratch
    near = lat.held.shape[0]
    g_near, g_far = grad_table()[:near, :], grad_table()[near:, :]
    p_near = (dot_t(g_near, ws()[...]) * slope_near()[...].astype(F32)).astype(BF)
    p_far = (dot_t(g_far, ws()[...]) * slope_far()[...].astype(F32)).astype(BF)
    fin = x_t.held.shape[0]
    tail = fin // 32 * 32
    g_embed[tail:, :] = jnp.zeros((g_embed.shape[0] - tail, g_embed.shape[1]), F32)
    g_embed[:fin, :] = dot(x_t()[...], p_near) + t_dot(x_far()[...], p_far)
    g_send[...] = t_dot(lat()[...], g_near) + t_dot(lat_far()[...], g_far)
    spread(me, order, (g_send, g_embed), *outs)


def collect_body(order, me, ins, outs, scratch):
    whole = scratch[0] if scratch else outs[0].held
    half = BLOCKS // 2
    deep = whole.shape[0] // BLOCKS
    for g, out in enumerate(outs):
        short = out.held.shape[0] != whole.shape[0]
        for place in range(BLOCKS):
            source = ins[place // half]()
            at = pl.multiple_of(block_of(place, me, order) * deep, deep)
            frm = ((place % half) * len(outs) + g) * deep
            (whole if short else out.held)[pl.ds(at, deep), :] = source[frm : frm + deep, :].astype(F32)
        if short:
            out.held[...] = whole[: out.held.shape[0], :]
        out.send()


def add_body(ins, outs, _):
    kept, got = ins
    total = kept()[...].astype(F32) + got()[...].astype(F32)
    deep = 0
    for out in outs:
        out.set(total[deep : deep + out.held.shape[0], :])
        deep += out.held.shape[0]


def join_body(ins, outs, _):
    half = ins[0].held.shape[0]
    outs[0].held[:half, :] = ins[0]()[...]
    outs[0].held[half:, :] = ins[1]()[...]


def load_body(ins, outs, _):
    for value in ins:
        value()


def exchange(value, step):
    n = lax.axis_size("space")
    return lax.ppermute(value, "space", [(i, i ^ step) for i in range(n)])


class Sum:
    def __init__(self, name, order, rest, keep, send, outs, scratch=()):
        self.name, self.order, self.outs, self.scratch = name, order, [(*v, "far") for v in outs], scratch
        halve = [("halve", order[i + 1]) for i in range(len(order) - 1)]
        whole = [("add", step) for step in (*rest, order[-1])]
        double = [("join", step) for step in order[-2::-1]]
        self.steps = halve + whole + double
        self.value, self.results = keep, None
        self.coming = exchange(send, order[0])

    def step(self, after, weight):
        rows, width = self.value.shape
        ins = [self.value, self.coming]
        if not self.steps:
            body = functools.partial(collect_body, self.order)
            self.results = call(body, f"{self.name}_collect", ins, self.outs, self.scratch, True, after, weight)
            return self.value
        kind, step = self.steps.pop(0)
        if kind == "halve":
            made = [((rows // 2, width), F32), ((rows // 2, width), BF)]
            self.value, sent = call(add_body, f"{self.name}_add", ins, made, after=after, weight=weight)
        else:
            body, made = (add_body, rows) if kind == "add" else (join_body, 2 * rows)
            (self.value,) = call(body, f"{self.name}_{kind}", ins, [((made, width), BF)], after=after, weight=weight)
            sent = self.value
        self.coming = exchange(sent, step)
        return self.value


def passed_along(block, distance):
    n = lax.axis_size("space")
    return lax.ppermute(block, "space", [((i - distance) % n, i) for i in range(n)])


def local(
    grid_inputs, mesh_latent, cotangent, send_list, enc_slot, enc_mask, halo_list, proc_slot, proc_mask,
    w_embed, enc_send, enc_recv, enc_out, proc_send, proc_recv, proc_out,
):
    n = lax.axis_size("space")
    rest = tuple(1 << i for i in range(3, n.bit_length() - 1))
    near, fin = grid_inputs.shape
    m, width = mesh_latent.shape
    edges_e = m * enc_slot.shape[1]
    edges_p = m * proc_slot.shape[1]
    depth = halo_list.shape[2]
    far = send_list.shape[1] * send_list.shape[2]
    x_t, sends_t, enc_slot_t, enc_mask_t, proc_slot_t, proc_mask_t = (
        v.T for v in (grid_inputs, send_list[0], enc_slot, enc_mask, proc_slot, proc_mask)
    )
    halo = halo_list[0]

    (outgoing,) = call(
        pick_body, "pick", [Far(sends_t), Far(x_t)], [((far, fin), BF, "far")], weight=FIRST[0]
    )
    incoming = lax.all_to_all(outgoing.reshape(n, -1, fin), "space", split_axis=0, concat_axis=0, tiled=True)
    x_far = incoming.reshape(far, fin)

    patch, edge_rows, patch_f32 = ((m, width), BF), ((depth, width), BF), ((m, width), F32)
    grid_rows, far_rows = ((near, width), BF), ((far, width), BF)
    lat, slope_near, proj, recv, w_embed, enc_send, latent, enc_out, proc_send, halo, enc_slot_t, enc_mask_t = call(
        embed_body,
        "embed",
        [Far(x_t), Kept(w_embed), Kept(enc_send), Kept(mesh_latent), Far(enc_recv), Kept(enc_out), Kept(proc_send),
         Kept(halo), Kept(enc_slot_t), Kept(enc_mask_t)],
        [(*grid_rows, "far"), (*grid_rows, "far"), grid_rows, patch_f32],
        weight=FIRST[1],
    )

    mid, to_left, to_right, mesh_proj, agg, y, r, slope, lat_far, slope_far = call(
        encode_body,
        "encode",
        [enc_slot_t, enc_mask_t, x_far, w_embed, enc_send, proj, recv, enc_out, latent, proc_send, halo],
        [patch, edge_rows, edge_rows, patch, patch, patch_f32, ((m, 128), F32), ((edges_e, width), BF), far_rows,
         far_rows],
        [((near + far, width), BF), ((edges_e, near + far), BF), ((edges_e, width), F32)],
    )

    from_left = passed_along(to_right, 1)
    from_right = passed_along(to_left, -1)

    after = (x_t, lat, slope_near, proc_recv, proc_out, cotangent, proc_slot_t, proc_mask_t, mid)
    x_t, lat, slope_near, proc_recv, proc_out, cotangent, proc_slot_t, proc_mask_t, mid = lax.optimization_barrier(after)
    x_t, lat, slope_near, proc_recv, proc_out, cotangent, proc_slot_t, proc_mask_t = call(
        load_body,
        "load",
        [Kept(v) for v in (x_t, lat, slope_near, proc_recv, proc_out, cotangent, proc_slot_t, proc_mask_t)],
        [],
        weight=FIRST[3],
    )

    wide = m + 2 * depth
    out, back_to_left, back_to_right, grad_rows, grad_mid, agg2, grad_u, grad_recv = call(
        process_body,
        "process",
        [proc_slot_t, proc_mask_t, mesh_proj, from_left, from_right, mid, proc_recv, proc_out, cotangent],
        [(*patch, "far"), edge_rows, edge_rows, patch_f32, patch_f32, patch, patch, patch],
        [((wide, width), BF), ((edges_p, wide), BF), ((wide, edges_p), BF), ((edges_p, width), F32),
         ((edges_p, width), F32), ((edges_p, width), BF)],
        weight=FIRST[4],
    )

    back_right = passed_along(back_to_left, -1)
    back_left = passed_along(back_to_right, 1)

    def halves(count):
        rows = count * width // 2
        return [((rows, width), F32), ((rows, width), BF)]

    square = ((width, width), F32)

    keep, send = call(
        functools.partial(process_grads_body, ORDER_P), "process_grads", [agg2, grad_u, mid, grad_recv], halves(2),
        [square] * 2, True, weight=FIRST[5],
    )
    sums = {"p": Sum("process", ORDER_P, rest, keep, send, [square] * 2)}
    token = keep
    for item in PLAN.split():
        item, weight = item[:-1], int(item[-1])
        if item == "mesh":
            keep, send, grad_table = call(
                functools.partial(mesh_grads_body, ORDER_M),
                "mesh_grads",
                [enc_slot_t, back_left, back_right, halo, grad_rows, proc_send, grad_mid, y, r, enc_out, slope, mid,
                 agg, latent],
                halves(3) + [((near + far, width), BF)],
                [((near + far, edges_e), BF), ((edges_e, width), BF)] + [square] * 3,
                True,
                token,
                weight,
            )
            token = keep
            sums["m"] = Sum("mesh", ORDER_M, rest, keep, send, [square] * 3)
        elif item == "grid":
            keep, send = call(
                functools.partial(grid_grads_body, ORDER_G),
                "grid_grads",
                [grad_table, enc_send, slope_near, slope_far, x_t, x_far, lat, lat_far],
                halves(2),
                [square] * 2,
                True,
                token,
                weight,
            )
            token = keep
            sums["g"] = Sum("grid", ORDER_G, rest, keep, send, [square, ((fin, width), F32)], [square])
        else:
            token = sums[item].step(token, weight)
    for total in sums.values():
        while total.results is None:
            token = total.step(token, 0)
    g_pout, g_precv = sums["p"].results
    g_psend, g_eout, g_erecv = sums["m"].results
    g_esend, g_embed = sums["g"].results
    return out, g_embed, g_esend, g_erecv, g_eout, g_psend, g_precv, g_pout


def solution(mesh):
    rows = P(("groups", "space"), None)
    lists = P(("groups", "space"), None, None)
    return jax.shard_map(
        local,
        mesh=mesh,
        in_specs=(rows, rows, rows, lists, rows, rows, lists, rows, rows) + (P(),) * 7,
        out_specs=(rows,) + (P("groups", None),) * 7,
        check_vma=False,
    )
```

```python
import functools

import jax
import jax.numpy as jnp
from jax import lax
from jax.experimental import pallas as pl
from jax.experimental.pallas import tpu as pltpu
from jax.sharding import PartitionSpec as P

BF = jnp.bfloat16
F32 = jnp.float32
VMEM_BYTES = 16 * 1024 * 1024
BLOCKS = 8
ORDER_P, ORDER_M, ORDER_G = (1, 2, 4), (1, 2, 4), (1, 4, 2)
PLAN = (("p", 3), ("mesh", 3), ("grid", 3), ("m", 3), ("p", 3), ("g", 3), ("p", 2), ("m", 3), ("g", 2), ("m", 3), ("p", 2), ("g", 3), ("p", 3), ("m", 3), ("g", 3), ("p", 3), ("m", 3), ("g", 3), ("p", 3), ("g", 3), ("m", 3), ("g", 4), ("m", 3))
WEIGHTS = (1, 10**9, 3 * 10**9, 10**10, 3 * 10**10, 10**11)
FIRST = (0, 0, 0, 0, 0, 0)


def dot(a, b):
    return lax.dot_general(a, b, (((1,), (0,)), ((), ())), preferred_element_type=F32)


def dot_t(a, b):
    return lax.dot_general(a, b, (((1,), (1,)), ((), ())), preferred_element_type=F32)


def t_dot(a, b):
    return lax.dot_general(a, b, (((0,), (0,)), ((), ())), preferred_element_type=F32)


def sigmoid(v):
    return 0.5 * jnp.tanh(0.5 * v) + 0.5


def silu_slope(v, s):
    return s * (1.0 + v * (1.0 - s))


def normalized(u):
    c = u - jnp.mean(u, axis=-1, keepdims=True)
    r = lax.rsqrt(jnp.mean(c * c, axis=-1, keepdims=True) + 1e-05)
    return c * r, r


def normalized_grad(y, r, g):
    return r * (g - jnp.mean(g, axis=-1, keepdims=True) - y * jnp.mean(g * y, axis=-1, keepdims=True))


class Far:
    def __init__(self, value):
        self.value = pltpu.with_memory_space_constraint(value, pltpu.HBM)
        self.shape, self.dtype = value.shape, value.dtype


class Kept:
    def __init__(self, value):
        self.value = pltpu.with_memory_space_constraint(value, pltpu.HBM)
        self.shape, self.dtype = value.shape, value.dtype


class Input:
    def __init__(self, source, held=None, sem=None):
        self.held, self.copy = source if held is None else held, None
        if held is not None:
            self.copy = pltpu.make_async_copy(source, held, sem)
            self.copy.start()

    def __call__(self):
        if self.copy is not None:
            self.copy.wait()
            self.copy = None
        return self.held


class Output:
    def __init__(self, target, held=None, sem=None):
        self.held, self.copy, self.started = target if held is None else held, None, False
        if held is not None:
            self.copy = pltpu.make_async_copy(held, target, sem)

    def send(self):
        if self.copy is not None:
            self.copy.start()
        self.started = True

    def set(self, value):
        self.held[...] = value.astype(self.held.dtype)
        self.send()


def call(body, name, ins, outs, scratch=(), place=False, after=None, weight=0):
    kept = [v for v in ins if isinstance(v, Kept)]
    far_in = [isinstance(v, (Far, Kept)) for v in ins]
    far_out = [len(v) > 2 for v in outs]
    n_in, n_out, n_kept = len(ins), len(outs), len(kept)
    lead = () if after is None else (after,)

    def kernel(*refs):
        refs = refs[len(lead) :]
        sources, targets = refs[:n_in], refs[n_in : n_in + n_out]
        kept_refs = list(refs[n_in + n_out : n_in + n_out + n_kept])
        rest = list(refs[n_in + n_out + n_kept :])
        out_sems, in_sems = rest.pop(), rest.pop()
        inputs, outputs = [], []
        for i, v in enumerate(ins):
            if isinstance(v, Kept):
                inputs.append(Input(sources[i], kept_refs.pop(0), in_sems.at[i]))
            elif isinstance(v, Far):
                inputs.append(Input(sources[i], rest.pop(0), in_sems.at[i]))
            else:
                inputs.append(Input(sources[i]))
        for i, is_far in enumerate(far_out):
            outputs.append(Output(targets[i], rest.pop(0), out_sems.at[i]) if is_far else Output(targets[i]))
        where = (lax.axis_index("space").astype(jnp.int32) & (BLOCKS - 1),) if place else ()
        body(*where, inputs, outputs, rest)
        for value in inputs:
            value()
        for value in outputs:
            if not value.started:
                value.send()
        for value in outputs:
            if value.copy is not None:
                value.copy.wait()

    anywhere, near = pl.BlockSpec(memory_space=pl.ANY), pl.BlockSpec(memory_space=pltpu.VMEM)
    held = [pltpu.VMEM(v.shape, v.dtype) for v in ins if isinstance(v, Far)]
    held += [pltpu.VMEM(v[0], v[1]) for v in outs if len(v) > 2]
    return pl.pallas_call(
        kernel,
        name=name,
        out_shape=[(pltpu.HBM if far else pltpu.VMEM)(v[0], v[1]) for v, far in zip(outs, far_out)]
        + [pltpu.VMEM(v.shape, v.dtype) for v in kept],
        in_specs=[anywhere] * len(lead) + [anywhere if far else near for far in far_in],
        out_specs=[anywhere if far else near for far in far_out] + [near] * n_kept,
        scratch_shapes=held
        + [pltpu.VMEM(shape, dtype) for shape, dtype in scratch]
        + [pltpu.SemaphoreType.DMA((n_in,)), pltpu.SemaphoreType.DMA((max(n_out, 1),))],
        compiler_params=pltpu.CompilerParams(vmem_limit_bytes=VMEM_BYTES),
        cost_estimate=pl.CostEstimate(flops=WEIGHTS[weight], bytes_accessed=1, transcendentals=0),
    )(*lead, *(v.value if far else v for v, far in zip(ins, far_in)))


def pick_body(ins, outs, _):
    sends_t, x_t = ins
    sends = sends_t()[...]
    cap, peers = sends.shape
    lanes = lax.broadcasted_iota(jnp.int32, (cap, x_t.held.shape[1]), 1)
    pick = [jnp.where(sends[:, d : d + 1] == lanes, 1.0, 0.0) for d in range(peers)]
    pick = jnp.concatenate(pick, axis=0).astype(BF)
    outs[0].set(dot_t(pick, x_t()[...]))


def embed_rows(pre, ws):
    s = sigmoid(pre)
    lat = (pre * s).astype(BF)
    return lat, silu_slope(pre, s).astype(BF), dot(lat, ws).astype(BF)


def embed_body(ins, outs, _):
    x_t, we, ws, latent, wrecv = ins[:5]
    lat, slope, proj, recv = outs
    x_t()
    at = t_dot(x_t()[...], we()[...])
    one, two, three = embed_rows(at, ws()[...])
    lat.set(one)
    slope.set(two)
    proj.set(three)
    recv.set(dot(latent()[...], wrecv()[...]))


def fill_onehot(onehot, slots):
    m, fan = slots.shape
    wide = onehot.shape[1]
    lanes = lax.broadcasted_iota(jnp.int32, (m, wide), 1)
    for f in range(fan):
        onehot[f * m : (f + 1) * m, :] = jnp.where(slots[:, f : f + 1] == lanes, 1.0, 0.0).astype(BF)


def fill_onehot_t(onehot, slots_t):
    fan, m = slots_t.shape
    tall = onehot.shape[0]
    subs = lax.broadcasted_iota(jnp.int32, (tall, 2 * m), 0)
    for f in range(0, fan, 2):
        pair = jnp.concatenate([slots_t[f : f + 1, :], slots_t[f + 1 : f + 2, :]], axis=1)
        onehot[:, f * m : (f + 2) * m] = jnp.where(pair == subs, 1.0, 0.0).astype(BF)


def messages(rows, recv, mask, slope):
    m, fan = mask.shape
    total = None
    for f in range(fan):
        at = slice(f * m, (f + 1) * m)
        v = rows[at, :] + recv
        s = sigmoid(v)
        k = mask[:, f : f + 1].astype(F32)
        slope[at, :] = (silu_slope(v, s) * k).astype(slope.dtype)
        part = v * s * k
        total = part if total is None else total + part
    return total.astype(BF)


def encode_body(ins, outs, scratch):
    slots_t, mask_t, x, we, ws, proj, recv, wout, latent, wnext, halo = ins
    mid, to_left, to_right, mesh_proj, agg, y, r, slope, lat_far, slope_far = outs
    table, onehot, rows = scratch
    near = proj.held.shape[0]
    fill_onehot(onehot, slots_t()[...].T)
    mask = mask_t()[...].T
    x()
    pre = dot(x()[...], we()[...])
    one, two, far = embed_rows(pre, ws()[...])
    lat_far.set(one)
    slope_far.set(two)
    table[near:, :] = far
    table[:near, :] = proj()[...]
    rows[...] = dot(onehot[...], table[...])
    summed = messages(rows, recv()[...], mask, slope.held)
    slope.send()
    agg.set(summed)
    normed, scale = normalized(dot(summed, wout()[...]))
    y.set(normed)
    r.set(jnp.broadcast_to(scale, r.held.shape))
    middle = (latent()[...].astype(F32) + normed).astype(BF)
    mid.set(middle)
    sent = dot(middle, wnext()[...]).astype(BF)
    mesh_proj.set(sent)
    lists = halo()[...]
    subs = lax.broadcasted_iota(jnp.int32, (sent.shape[0], lists.shape[1]), 0)
    to_left.set(t_dot(jnp.where(lists[0:1, :] == subs, 1.0, 0.0).astype(BF), sent))
    to_right.set(t_dot(jnp.where(lists[1:2, :] == subs, 1.0, 0.0).astype(BF), sent))


def process_body(ins, outs, scratch):
    slots_t, mask_t, mesh_proj, left, right, mid, wrecv, wout, cotangent = ins
    out, to_left, to_right, grad_rows, grad_mid, agg, grad_u, grad_recv = outs
    table, onehot, onehot_t, rows, slope, grad_msg = scratch
    m = mesh_proj.held.shape[0]
    depth = left.held.shape[0]
    slots = slots_t()[...]
    fill_onehot(onehot, slots.T)
    mask = mask_t()[...].T
    fill_onehot_t(onehot_t, slots)
    table[:m, :] = mesh_proj()[...]
    table[m : m + depth, :] = left()[...]
    table[m + depth : m + 2 * depth, :] = right()[...]
    rows[...] = dot(onehot[...], table[...])
    middle = mid()[...]
    summed = messages(rows, dot(middle, wrecv()[...]), mask, slope)
    agg.set(summed)
    normed, scale = normalized(dot(summed, wout()[...]))
    out.set(middle.astype(F32) + normed)
    ct = cotangent()[...].astype(F32)
    gu = normalized_grad(normed, scale, ct).astype(BF)
    grad_u.set(gu)
    gr = message_grads(grad_msg, slope, dot_t(gu, wout()[...]), mask.shape[1])
    grad_recv.set(gr)
    grads = dot(onehot_t[...], grad_msg[...])
    to_left.set(grads[m : m + depth, :])
    to_right.set(grads[m + depth :, :])
    grad_rows.set(grads[:m, :])
    grad_mid.set(ct + dot_t(gr, wrecv()[...]))


def message_grads(grad_msg, slope, gagg, fan):
    m = gagg.shape[0]
    total = None
    for f in range(fan):
        at = slice(f * m, (f + 1) * m)
        g = slope[at, :].astype(F32) * gagg
        grad_msg[at, :] = g.astype(BF)
        total = g if total is None else total + g
    return total.astype(BF)


def block_of(place, me, order):
    flips = 0
    for i, step in enumerate(order):
        if place >> (len(order) - 1 - i) & 1:
            flips ^= step
    return me ^ flips


def spread(me, order, grads, keep, send):
    deep = grads[0].shape[0] // BLOCKS
    half = BLOCKS // 2
    for place in reversed(range(BLOCKS)):
        at = pl.multiple_of(block_of(place, me, order) * deep, deep)
        for g, grad in enumerate(grads):
            to = ((place % half) * len(grads) + g) * deep
            target = keep if place < half else send
            target.held[to : to + deep, :] = grad[pl.ds(at, deep), :].astype(target.held.dtype)
        if place == half:
            send.send()
    keep.send()


def process_grads_body(order, me, ins, outs, scratch):
    agg, grad_u, mid, grad_recv = ins
    one, two = scratch
    one[...] = t_dot(agg()[...], grad_u()[...])
    two[...] = t_dot(mid()[...], grad_recv()[...])
    spread(me, order, (one, two), *outs)


def mesh_grads_body(order, me, ins, outs, scratch):
    slots_t, back_left, back_right, halo, grad_rows, wnext, grad_mid, y, r, wout, slope, mid, agg, latent = ins
    keep, send, grad_table = outs
    onehot_t, grad_msg, g_next, g_out, g_recv = scratch
    m = mid.held.shape[0]
    fill_onehot_t(onehot_t, slots_t()[...])
    lists = halo()[...]
    subs = lax.broadcasted_iota(jnp.int32, (m, lists.shape[1]), 0)
    to_left = jnp.where(lists[0:1, :] == subs, 1.0, 0.0).astype(BF)
    to_right = jnp.where(lists[1:2, :] == subs, 1.0, 0.0).astype(BF)
    gp = (grad_rows()[...] + dot(to_right, back_right()[...]) + dot(to_left, back_left()[...])).astype(BF)
    gmid = grad_mid()[...] + dot_t(gp, wnext()[...])
    gu = normalized_grad(y()[...], r()[:, 0:1], gmid).astype(BF)
    gagg = dot_t(gu, wout()[...])
    gr = message_grads(grad_msg, slope(), gagg, grad_msg.shape[0] // m)
    grad_table.set(dot(onehot_t[...], grad_msg[...]))
    g_next[...] = t_dot(mid()[...], gp)
    g_out[...] = t_dot(agg()[...], gu)
    g_recv[...] = t_dot(latent()[...], gr)
    spread(me, order, (g_next, g_out, g_recv), keep, send)


def grid_grads_body(order, me, ins, outs, scratch):
    grad_table, ws, slope_near, slope_far, x_t, x_far, lat, lat_far = ins
    g_send, g_embed = scratch
    near = lat.held.shape[0]
    g_near, g_far = grad_table()[:near, :], grad_table()[near:, :]
    p_near = (dot_t(g_near, ws()[...]) * slope_near()[...].astype(F32)).astype(BF)
    p_far = (dot_t(g_far, ws()[...]) * slope_far()[...].astype(F32)).astype(BF)
    fin = x_t.held.shape[0]
    tail = fin // 32 * 32
    g_embed[tail:, :] = jnp.zeros((g_embed.shape[0] - tail, g_embed.shape[1]), F32)
    g_embed[:fin, :] = dot(x_t()[...], p_near) + t_dot(x_far()[...], p_far)
    g_send[...] = t_dot(lat()[...], g_near) + t_dot(lat_far()[...], g_far)
    spread(me, order, (g_send, g_embed), *outs)


def collect_body(order, me, ins, outs, scratch):
    whole = scratch[0] if scratch else outs[0].held
    half = BLOCKS // 2
    deep = whole.shape[0] // BLOCKS
    for g, out in enumerate(outs):
        short = out.held.shape[0] != whole.shape[0]
        for place in range(BLOCKS):
            source = ins[place // half]()
            at = pl.multiple_of(block_of(place, me, order) * deep, deep)
            frm = ((place % half) * len(outs) + g) * deep
            (whole if short else out.held)[pl.ds(at, deep), :] = source[frm : frm + deep, :].astype(F32)
        if short:
            out.held[...] = whole[: out.held.shape[0], :]
        out.send()


def add_body(ins, outs, _):
    kept, got = ins
    total = kept()[...].astype(F32) + got()[...].astype(F32)
    deep = 0
    for out in outs:
        out.set(total[deep : deep + out.held.shape[0], :])
        deep += out.held.shape[0]


def join_body(ins, outs, _):
    half = ins[0].held.shape[0]
    outs[0].held[:half, :] = ins[0]()[...]
    outs[0].held[half:, :] = ins[1]()[...]


def load_body(ins, outs, _):
    for value in ins:
        value()


def exchange(value, step):
    n = lax.axis_size("space")
    return lax.ppermute(value, "space", [(i, i ^ step) for i in range(n)])


class Sum:
    def __init__(self, name, order, rest, keep, send, outs, scratch=()):
        self.name, self.order, self.outs, self.scratch = name, order, [(*v, "far") for v in outs], scratch
        halve = [("halve", order[i + 1]) for i in range(len(order) - 1)]
        whole = [("add", step) for step in (*rest, order[-1])]
        double = [("join", step) for step in order[-2::-1]]
        self.steps = halve + whole + double
        self.value, self.results = keep, None
        self.coming = exchange(send, order[0])

    def step(self, after, weight):
        rows, width = self.value.shape
        ins = [self.value, self.coming]
        if not self.steps:
            body = functools.partial(collect_body, self.order)
            self.results = call(body, f"{self.name}_collect", ins, self.outs, self.scratch, True, after, weight)
            return pltpu.with_memory_space_constraint(self.results[0], pltpu.HBM)
        kind, step = self.steps.pop(0)
        if kind == "halve":
            made = [((rows // 2, width), F32), ((rows // 2, width), BF)]
            self.value, sent = call(add_body, f"{self.name}_add", ins, made, after=after, weight=weight)
        else:
            body, made = (add_body, rows) if kind == "add" else (join_body, 2 * rows)
            (self.value,) = call(body, f"{self.name}_{kind}", ins, [((made, width), BF)], after=after, weight=weight)
            sent = self.value
        self.coming = exchange(sent, step)
        return self.value


def passed_along(block, distance):
    n = lax.axis_size("space")
    return lax.ppermute(block, "space", [((i - distance) % n, i) for i in range(n)])


def local(
    grid_inputs, mesh_latent, cotangent, send_list, enc_slot, enc_mask, halo_list, proc_slot, proc_mask,
    w_embed, enc_send, enc_recv, enc_out, proc_send, proc_recv, proc_out,
):
    n = lax.axis_size("space")
    rest = tuple(1 << i for i in range(3, n.bit_length() - 1))
    near, fin = grid_inputs.shape
    m, width = mesh_latent.shape
    edges_e = m * enc_slot.shape[1]
    edges_p = m * proc_slot.shape[1]
    depth = halo_list.shape[2]
    far = send_list.shape[1] * send_list.shape[2]
    x_t, sends_t, enc_slot_t, enc_mask_t, proc_slot_t, proc_mask_t = (
        v.T for v in (grid_inputs, send_list[0], enc_slot, enc_mask, proc_slot, proc_mask)
    )
    halo = halo_list[0]

    (outgoing,) = call(
        pick_body, "pick", [Far(sends_t), Far(x_t)], [((far, fin), BF, "far")], weight=FIRST[0]
    )
    incoming = lax.all_to_all(outgoing.reshape(n, -1, fin), "space", split_axis=0, concat_axis=0, tiled=True)
    x_far = incoming.reshape(far, fin)

    patch, edge_rows, patch_f32 = ((m, width), BF), ((depth, width), BF), ((m, width), F32)
    grid_rows, far_rows = ((near, width), BF), ((far, width), BF)
    lat, slope_near, proj, recv, w_embed, enc_send, latent, enc_out, proc_send, halo, enc_slot_t, enc_mask_t = call(
        embed_body,
        "embed",
        [Far(x_t), Kept(w_embed), Kept(enc_send), Kept(mesh_latent), Far(enc_recv), Kept(enc_out), Kept(proc_send),
         Kept(halo), Kept(enc_slot_t), Kept(enc_mask_t)],
        [(*grid_rows, "far"), (*grid_rows, "far"), grid_rows, patch_f32],
        weight=FIRST[1],
    )

    mid, to_left, to_right, mesh_proj, agg, y, r, slope, lat_far, slope_far = call(
        encode_body,
        "encode",
        [enc_slot_t, enc_mask_t, x_far, w_embed, enc_send, proj, recv, enc_out, latent, proc_send, halo],
        [patch, edge_rows, edge_rows, patch, patch, patch_f32, ((m, 128), F32), ((edges_e, width), BF), far_rows,
         far_rows],
        [((near + far, width), BF), ((edges_e, near + far), BF), ((edges_e, width), F32)],
    )

    from_left = passed_along(to_right, 1)
    from_right = passed_along(to_left, -1)

    after = (x_t, lat, slope_near, proc_recv, proc_out, cotangent, proc_slot_t, proc_mask_t, mid)
    x_t, lat, slope_near, proc_recv, proc_out, cotangent, proc_slot_t, proc_mask_t, mid = lax.optimization_barrier(after)
    x_t, lat, slope_near, proc_recv, proc_out, cotangent, proc_slot_t, proc_mask_t = call(
        load_body,
        "load",
        [Kept(v) for v in (x_t, lat, slope_near, proc_recv, proc_out, cotangent, proc_slot_t, proc_mask_t)],
        [],
        weight=FIRST[3],
    )

    wide = m + 2 * depth
    out, back_to_left, back_to_right, grad_rows, grad_mid, agg2, grad_u, grad_recv = call(
        process_body,
        "process",
        [proc_slot_t, proc_mask_t, mesh_proj, from_left, from_right, mid, proc_recv, proc_out, cotangent],
        [(*patch, "far"), edge_rows, edge_rows, patch_f32, patch_f32, patch, patch, patch],
        [((wide, width), BF), ((edges_p, wide), BF), ((wide, edges_p), BF), ((edges_p, width), F32),
         ((edges_p, width), F32), ((edges_p, width), BF)],
        weight=FIRST[4],
    )

    back_right = passed_along(back_to_left, -1)
    back_left = passed_along(back_to_right, 1)

    def halves(count):
        rows = count * width // 2
        return [((rows, width), F32), ((rows, width), BF)]

    square = ((width, width), F32)

    keep, send = call(
        functools.partial(process_grads_body, ORDER_P), "process_grads", [agg2, grad_u, mid, grad_recv], halves(2),
        [square] * 2, True, weight=FIRST[5],
    )
    sums = {"p": Sum("process", ORDER_P, rest, keep, send, [square] * 2)}
    token = keep
    for item, weight in PLAN:
        if item == "mesh":
            keep, send, grad_table = call(
                functools.partial(mesh_grads_body, ORDER_M),
                "mesh_grads",
                [enc_slot_t, back_left, back_right, halo, grad_rows, proc_send, grad_mid, y, r, enc_out, slope, mid,
                 agg, latent],
                halves(3) + [((near + far, width), BF)],
                [((near + far, edges_e), BF), ((edges_e, width), BF)] + [square] * 3,
                True,
                token,
                weight,
            )
            token = keep
            sums["m"] = Sum("mesh", ORDER_M, rest, keep, send, [square] * 3)
        elif item == "grid":
            keep, send = call(
                functools.partial(grid_grads_body, ORDER_G),
                "grid_grads",
                [grad_table, enc_send, slope_near, slope_far, x_t, x_far, lat, lat_far],
                halves(2),
                [square] * 2,
                True,
                token,
                weight,
            )
            token = keep
            sums["g"] = Sum("grid", ORDER_G, rest, keep, send, [square, ((fin, width), F32)], [square])
        else:
            token = sums[item].step(token, weight)
    for total in sums.values():
        while total.results is None:
            token = total.step(token, 0)
    g_pout, g_precv = sums["p"].results
    g_psend, g_eout, g_erecv = sums["m"].results
    g_esend, g_embed = sums["g"].results
    return out, g_embed, g_esend, g_erecv, g_eout, g_psend, g_precv, g_pout


def solution(mesh):
    rows = P(("groups", "space"), None)
    lists = P(("groups", "space"), None, None)
    return jax.shard_map(
        local,
        mesh=mesh,
        in_specs=(rows, rows, rows, lists, rows, rows, lists, rows, rows) + (P(),) * 7,
        out_specs=(rows,) + (P("groups", None),) * 7,
        check_vma=False,
    )
```

```python
import functools

import jax
import jax.numpy as jnp
from jax import lax
from jax.experimental import pallas as pl
from jax.experimental.pallas import tpu as pltpu
from jax.sharding import PartitionSpec as P

BF = jnp.bfloat16
F32 = jnp.float32
VMEM_BYTES = 16 * 1024 * 1024
BLOCKS = 8
ORDER_P, ORDER_M, ORDER_G = (1, 2, 4), (1, 2, 4), (1, 4, 2)
PLAN = (("p", 3), ("mesh", 3), ("grid", 3), ("m", 3), ("p", 3), ("g", 3), ("p", 2), ("m", 3), ("g", 2), ("m", 3), ("p", 2), ("g", 3), ("p", 3), ("m", 3), ("g", 3), ("p", 3), ("m", 3), ("g", 3), ("p", 3), ("g", 3), ("m", 3), ("g", 4), ("m", 3))
WEIGHTS = (1, 10**9, 3 * 10**9, 10**10, 3 * 10**10, 10**11)
FIRST = (0, 0, 0, 0, 0, 0)


def dot(a, b):
    return lax.dot_general(a, b, (((1,), (0,)), ((), ())), preferred_element_type=F32)


def dot_t(a, b):
    return lax.dot_general(a, b, (((1,), (1,)), ((), ())), preferred_element_type=F32)


def t_dot(a, b):
    return lax.dot_general(a, b, (((0,), (0,)), ((), ())), preferred_element_type=F32)


def sigmoid(v):
    return 0.5 * jnp.tanh(0.5 * v) + 0.5


def silu_slope(v, s):
    return s * (1.0 + v * (1.0 - s))


def normalized(u):
    c = u - jnp.mean(u, axis=-1, keepdims=True)
    r = lax.rsqrt(jnp.mean(c * c, axis=-1, keepdims=True) + 1e-05)
    return c * r, r


def normalized_grad(y, r, g):
    return r * (g - jnp.mean(g, axis=-1, keepdims=True) - y * jnp.mean(g * y, axis=-1, keepdims=True))


class Far:
    def __init__(self, value):
        self.value = pltpu.with_memory_space_constraint(value, pltpu.HBM)
        self.shape, self.dtype = value.shape, value.dtype


class Kept:
    def __init__(self, value):
        self.value = pltpu.with_memory_space_constraint(value, pltpu.HBM)
        self.shape, self.dtype = value.shape, value.dtype


class Input:
    def __init__(self, source, held=None, sem=None):
        self.held, self.copy = source if held is None else held, None
        if held is not None:
            self.copy = pltpu.make_async_copy(source, held, sem)
            self.copy.start()

    def __call__(self):
        if self.copy is not None:
            self.copy.wait()
            self.copy = None
        return self.held


class Output:
    def __init__(self, target, held=None, sem=None):
        self.held, self.copy, self.started = target if held is None else held, None, False
        if held is not None:
            self.copy = pltpu.make_async_copy(held, target, sem)

    def send(self):
        if self.copy is not None:
            self.copy.start()
        self.started = True

    def set(self, value):
        self.held[...] = value.astype(self.held.dtype)
        self.send()


def call(body, name, ins, outs, scratch=(), place=False, after=None, weight=0):
    kept = [v for v in ins if isinstance(v, Kept)]
    far_in = [isinstance(v, (Far, Kept)) for v in ins]
    far_out = [len(v) > 2 for v in outs]
    n_in, n_out, n_kept = len(ins), len(outs), len(kept)
    lead = () if after is None else (after,)

    def kernel(*refs):
        refs = refs[len(lead) :]
        sources, targets = refs[:n_in], refs[n_in : n_in + n_out]
        kept_refs = list(refs[n_in + n_out : n_in + n_out + n_kept])
        rest = list(refs[n_in + n_out + n_kept :])
        out_sems, in_sems = rest.pop(), rest.pop()
        inputs, outputs = [], []
        for i, v in enumerate(ins):
            if isinstance(v, Kept):
                inputs.append(Input(sources[i], kept_refs.pop(0), in_sems.at[i]))
            elif isinstance(v, Far):
                inputs.append(Input(sources[i], rest.pop(0), in_sems.at[i]))
            else:
                inputs.append(Input(sources[i]))
        for i, is_far in enumerate(far_out):
            outputs.append(Output(targets[i], rest.pop(0), out_sems.at[i]) if is_far else Output(targets[i]))
        where = (lax.axis_index("space").astype(jnp.int32),) if place else ()
        body(*where, inputs, outputs, rest)
        for value in inputs:
            value()
        for value in outputs:
            if not value.started:
                value.send()
        for value in outputs:
            if value.copy is not None:
                value.copy.wait()

    anywhere, near = pl.BlockSpec(memory_space=pl.ANY), pl.BlockSpec(memory_space=pltpu.VMEM)
    held = [pltpu.VMEM(v.shape, v.dtype) for v in ins if isinstance(v, Far)]
    held += [pltpu.VMEM(v[0], v[1]) for v in outs if len(v) > 2]
    return pl.pallas_call(
        kernel,
        name=name,
        out_shape=[(pltpu.HBM if far else pltpu.VMEM)(v[0], v[1]) for v, far in zip(outs, far_out)]
        + [pltpu.VMEM(v.shape, v.dtype) for v in kept],
        in_specs=[anywhere] * len(lead) + [anywhere if far else near for far in far_in],
        out_specs=[anywhere if far else near for far in far_out] + [near] * n_kept,
        scratch_shapes=held
        + [pltpu.VMEM(shape, dtype) for shape, dtype in scratch]
        + [pltpu.SemaphoreType.DMA((n_in,)), pltpu.SemaphoreType.DMA((max(n_out, 1),))],
        compiler_params=pltpu.CompilerParams(vmem_limit_bytes=VMEM_BYTES),
        cost_estimate=pl.CostEstimate(flops=WEIGHTS[weight], bytes_accessed=1, transcendentals=0),
    )(*lead, *(v.value if far else v for v, far in zip(ins, far_in)))


def pick_body(ins, outs, _):
    sends_t, x_t = ins
    sends = sends_t()[...]
    cap, peers = sends.shape
    lanes = lax.broadcasted_iota(jnp.int32, (cap, x_t.held.shape[1]), 1)
    pick = [jnp.where(sends[:, d : d + 1] == lanes, 1.0, 0.0) for d in range(peers)]
    pick = jnp.concatenate(pick, axis=0).astype(BF)
    outs[0].set(dot_t(pick, x_t()[...]))


def embed_rows(pre, ws):
    s = sigmoid(pre)
    lat = (pre * s).astype(BF)
    return lat, silu_slope(pre, s).astype(BF), dot(lat, ws).astype(BF)


def embed_body(ins, outs, _):
    x_t, we, ws, latent, wrecv = ins[:5]
    lat, slope, proj, recv = outs
    x_t()
    at = t_dot(x_t()[...], we()[...])
    one, two, three = embed_rows(at, ws()[...])
    lat.set(one)
    slope.set(two)
    proj.set(three)
    recv.set(dot(latent()[...], wrecv()[...]))


def fill_onehot(onehot, slots):
    m, fan = slots.shape
    wide = onehot.shape[1]
    lanes = lax.broadcasted_iota(jnp.int32, (m, wide), 1)
    for f in range(fan):
        onehot[f * m : (f + 1) * m, :] = jnp.where(slots[:, f : f + 1] == lanes, 1.0, 0.0).astype(BF)


def fill_onehot_t(onehot, slots_t):
    fan, m = slots_t.shape
    tall = onehot.shape[0]
    subs = lax.broadcasted_iota(jnp.int32, (tall, 2 * m), 0)
    for f in range(0, fan, 2):
        pair = jnp.concatenate([slots_t[f : f + 1, :], slots_t[f + 1 : f + 2, :]], axis=1)
        onehot[:, f * m : (f + 2) * m] = jnp.where(pair == subs, 1.0, 0.0).astype(BF)


def messages(rows, recv, mask, slope):
    m, fan = mask.shape
    total = None
    for f in range(fan):
        at = slice(f * m, (f + 1) * m)
        v = rows[at, :] + recv
        s = sigmoid(v)
        k = mask[:, f : f + 1].astype(F32)
        slope[at, :] = (silu_slope(v, s) * k).astype(slope.dtype)
        part = v * s * k
        total = part if total is None else total + part
    return total.astype(BF)


def encode_body(me, ins, outs, scratch):
    slots_t, mask_t, x, we, ws, proj, recv, wout, latent, wnext, halo = ins
    mid, one, two, mesh_proj, agg, y, r, slope, lat_far, slope_far = outs
    table, onehot, rows = scratch
    near = proj.held.shape[0]
    fill_onehot(onehot, slots_t()[...].T)
    mask = mask_t()[...].T
    x()
    pre = dot(x()[...], we()[...])
    lat, bend, far = embed_rows(pre, ws()[...])
    lat_far.set(lat)
    slope_far.set(bend)
    table[near:, :] = far
    table[:near, :] = proj()[...]
    rows[...] = dot(onehot[...], table[...])
    summed = messages(rows, recv()[...], mask, slope.held)
    slope.send()
    agg.set(summed)
    normed, scale = normalized(dot(summed, wout()[...]))
    y.set(normed)
    r.set(jnp.broadcast_to(scale, r.held.shape))
    middle = (latent()[...].astype(F32) + normed).astype(BF)
    mid.set(middle)
    sent = dot(middle, wnext()[...]).astype(BF)
    mesh_proj.set(sent)
    lists = halo()[...]
    subs = lax.broadcasted_iota(jnp.int32, (sent.shape[0], lists.shape[1]), 0)
    odd = 1 - me % 2
    for out, towards in ((one, 1 - odd), (two, odd)):
        rows = jnp.where(towards == 0, lists[0:1, :], lists[1:2, :])
        out.set(t_dot(jnp.where(rows == subs, 1.0, 0.0).astype(BF), sent))


def process_body(me, ins, outs, scratch):
    slots_t, mask_t, mesh_proj, one, two, mid, wrecv, wout, cotangent = ins
    out, back_one, back_two, grad_rows, grad_mid, agg, grad_u, grad_recv = outs
    table, onehot, onehot_t, rows, slope, grad_msg = scratch
    m = mesh_proj.held.shape[0]
    depth = one.held.shape[0]
    odd = me % 2 == 0
    slots = slots_t()[...]
    fill_onehot(onehot, slots.T)
    mask = mask_t()[...].T
    fill_onehot_t(onehot_t, slots)
    table[:m, :] = mesh_proj()[...]
    from_one, from_two = one()[...], two()[...]
    table[m : m + depth, :] = jnp.where(odd, from_one, from_two)
    table[m + depth : m + 2 * depth, :] = jnp.where(odd, from_two, from_one)
    rows[...] = dot(onehot[...], table[...])
    middle = mid()[...]
    summed = messages(rows, dot(middle, wrecv()[...]), mask, slope)
    agg.set(summed)
    normed, scale = normalized(dot(summed, wout()[...]))
    out.set(middle.astype(F32) + normed)
    ct = cotangent()[...].astype(F32)
    gu = normalized_grad(normed, scale, ct).astype(BF)
    grad_u.set(gu)
    gr = message_grads(grad_msg, slope, dot_t(gu, wout()[...]), mask.shape[1])
    grad_recv.set(gr)
    grads = dot(onehot_t[...], grad_msg[...])
    to_left, to_right = grads[m : m + depth, :], grads[m + depth :, :]
    back_one.set(jnp.where(odd, to_left, to_right))
    back_two.set(jnp.where(odd, to_right, to_left))
    grad_rows.set(grads[:m, :])
    grad_mid.set(ct + dot_t(gr, wrecv()[...]))


def message_grads(grad_msg, slope, gagg, fan):
    m = gagg.shape[0]
    total = None
    for f in range(fan):
        at = slice(f * m, (f + 1) * m)
        g = slope[at, :].astype(F32) * gagg
        grad_msg[at, :] = g.astype(BF)
        total = g if total is None else total + g
    return total.astype(BF)


def block_of(place, me, order):
    flips = 0
    for i, step in enumerate(order):
        if place >> (len(order) - 1 - i) & 1:
            flips ^= step
    return (me & (BLOCKS - 1)) ^ flips


def spread(me, order, grads, keep, send):
    deep = grads[0].shape[0] // BLOCKS
    half = BLOCKS // 2
    for place in reversed(range(BLOCKS)):
        at = pl.multiple_of(block_of(place, me, order) * deep, deep)
        for g, grad in enumerate(grads):
            to = ((place % half) * len(grads) + g) * deep
            target = keep if place < half else send
            target.held[to : to + deep, :] = grad[pl.ds(at, deep), :].astype(target.held.dtype)
        if place == half:
            send.send()
    keep.send()


def process_grads_body(order, me, ins, outs, scratch):
    agg, grad_u, mid, grad_recv = ins
    one, two = scratch
    one[...] = t_dot(agg()[...], grad_u()[...])
    two[...] = t_dot(mid()[...], grad_recv()[...])
    spread(me, order, (one, two), *outs)


def mesh_grads_body(order, me, ins, outs, scratch):
    back_one, back_two, halo, grad_rows, wnext, grad_mid, y, r, wout, slope, mid, agg, latent = ins
    keep, send, grad_msg = outs
    g_next, g_out, g_recv = scratch
    m = mid.held.shape[0]
    lists = halo()[...]
    subs = lax.broadcasted_iota(jnp.int32, (m, lists.shape[1]), 0)
    odd = me % 2 == 0
    put_one = jnp.where(jnp.where(odd, lists[0:1, :], lists[1:2, :]) == subs, 1.0, 0.0).astype(BF)
    put_two = jnp.where(jnp.where(odd, lists[1:2, :], lists[0:1, :]) == subs, 1.0, 0.0).astype(BF)
    gp = (grad_rows()[...] + dot(put_one, back_one()[...]) + dot(put_two, back_two()[...])).astype(BF)
    gmid = grad_mid()[...] + dot_t(gp, wnext()[...])
    gu = normalized_grad(y()[...], r()[:, 0:1], gmid).astype(BF)
    gagg = dot_t(gu, wout()[...])
    gr = message_grads(grad_msg.held, slope(), gagg, grad_msg.held.shape[0] // m)
    g_next[...] = t_dot(mid()[...], gp)
    g_out[...] = t_dot(agg()[...], gu)
    g_recv[...] = t_dot(latent()[...], gr)
    spread(me, order, (g_next, g_out, g_recv), keep, send)


def grid_grads_body(order, me, ins, outs, scratch):
    slots_t, grad_msg, ws, slope_near, slope_far, x_t, x_far, lat, lat_far = ins
    onehot_t, g_send, g_embed = scratch
    near = lat.held.shape[0]
    fill_onehot_t(onehot_t, slots_t()[...])
    grad_table = dot(onehot_t[...], grad_msg()[...]).astype(BF)
    g_near, g_far = grad_table[:near, :], grad_table[near:, :]
    p_near = (dot_t(g_near, ws()[...]) * slope_near()[...].astype(F32)).astype(BF)
    p_far = (dot_t(g_far, ws()[...]) * slope_far()[...].astype(F32)).astype(BF)
    fin = x_t.held.shape[0]
    tail = fin // 32 * 32
    g_embed[tail:, :] = jnp.zeros((g_embed.shape[0] - tail, g_embed.shape[1]), F32)
    g_embed[:fin, :] = dot(x_t()[...], p_near) + t_dot(x_far()[...], p_far)
    g_send[...] = t_dot(lat()[...], g_near) + t_dot(lat_far()[...], g_far)
    spread(me, order, (g_send, g_embed), *outs)


def collect_body(order, me, ins, outs, scratch):
    whole = scratch[0] if scratch else outs[0].held
    half = BLOCKS // 2
    deep = whole.shape[0] // BLOCKS
    for g, out in enumerate(outs):
        short = out.held.shape[0] != whole.shape[0]
        for place in range(BLOCKS):
            source = ins[place // half]()
            at = pl.multiple_of(block_of(place, me, order) * deep, deep)
            frm = ((place % half) * len(outs) + g) * deep
            (whole if short else out.held)[pl.ds(at, deep), :] = source[frm : frm + deep, :].astype(F32)
        if short:
            out.held[...] = whole[: out.held.shape[0], :]
        out.send()


def add_body(ins, outs, _):
    kept, got = ins
    total = kept()[...].astype(F32) + got()[...].astype(F32)
    deep = 0
    for out in outs:
        out.set(total[deep : deep + out.held.shape[0], :])
        deep += out.held.shape[0]


def join_body(ins, outs, _):
    half = ins[0].held.shape[0]
    outs[0].held[:half, :] = ins[0]()[...]
    outs[0].held[half:, :] = ins[1]()[...]


def load_body(ins, outs, _):
    for value in ins:
        value()


def exchange(value, step):
    n = lax.axis_size("space")
    return lax.ppermute(value, "space", [(i, i ^ step) for i in range(n)])


class Sum:
    def __init__(self, name, order, rest, keep, send, outs, scratch=()):
        self.name, self.order, self.outs, self.scratch = name, order, [(*v, "far") for v in outs], scratch
        halve = [("halve", order[i + 1]) for i in range(len(order) - 1)]
        whole = [("add", step) for step in (*rest, order[-1])]
        double = [("join", step) for step in order[-2::-1]]
        self.steps = halve + whole + double
        self.value, self.results = keep, None
        self.coming = exchange(send, order[0])

    def step(self, after, weight):
        rows, width = self.value.shape
        ins = [self.value, self.coming]
        if not self.steps:
            body = functools.partial(collect_body, self.order)
            self.results = call(body, f"{self.name}_collect", ins, self.outs, self.scratch, True, after, weight)
            return pltpu.with_memory_space_constraint(self.results[0], pltpu.HBM)
        kind, step = self.steps.pop(0)
        if kind == "halve":
            made = [((rows // 2, width), F32), ((rows // 2, width), BF)]
            self.value, sent = call(add_body, f"{self.name}_add", ins, made, after=after, weight=weight)
        else:
            body, made = (add_body, rows) if kind == "add" else (join_body, 2 * rows)
            (self.value,) = call(body, f"{self.name}_{kind}", ins, [((made, width), BF)], after=after, weight=weight)
            sent = self.value
        self.coming = exchange(sent, step)
        return self.value


def swapped(rows, first):
    n = lax.axis_size("space")
    pairs = [((first + i) % n, (first + i + 1) % n) for i in range(0, n, 2)]
    return lax.ppermute(rows, "space", [*pairs, *((b, a) for a, b in pairs)])


def local(
    grid_inputs, mesh_latent, cotangent, send_list, enc_slot, enc_mask, halo_list, proc_slot, proc_mask,
    w_embed, enc_send, enc_recv, enc_out, proc_send, proc_recv, proc_out,
):
    n = lax.axis_size("space")
    rest = tuple(1 << i for i in range(3, n.bit_length() - 1))
    near, fin = grid_inputs.shape
    m, width = mesh_latent.shape
    edges_e = m * enc_slot.shape[1]
    edges_p = m * proc_slot.shape[1]
    depth = halo_list.shape[2]
    far = send_list.shape[1] * send_list.shape[2]
    x_t, sends_t, enc_slot_t, enc_mask_t, proc_slot_t, proc_mask_t = (
        v.T for v in (grid_inputs, send_list[0], enc_slot, enc_mask, proc_slot, proc_mask)
    )
    halo = halo_list[0]

    (outgoing,) = call(
        pick_body, "pick", [Far(sends_t), Far(x_t)], [((far, fin), BF)], weight=FIRST[0]
    )
    incoming = lax.all_to_all(outgoing.reshape(n, -1, fin), "space", split_axis=0, concat_axis=0, tiled=True)
    x_far = incoming.reshape(far, fin)

    patch, edge_rows, patch_f32 = ((m, width), BF), ((depth, width), BF), ((m, width), F32)
    grid_rows, far_rows = ((near, width), BF), ((far, width), BF)
    lat, slope_near, proj, recv, w_embed, enc_send, latent, enc_out, proc_send, halo, enc_slot_t, enc_mask_t = call(
        embed_body,
        "embed",
        [Far(x_t), Kept(w_embed), Kept(enc_send), Kept(mesh_latent), Far(enc_recv), Kept(enc_out), Kept(proc_send),
         Kept(halo), Kept(enc_slot_t), Kept(enc_mask_t)],
        [(*grid_rows, "far"), (*grid_rows, "far"), grid_rows, patch_f32],
        weight=FIRST[1],
    )

    mid, to_one, to_two, mesh_proj, agg, y, r, slope, lat_far, slope_far = call(
        encode_body,
        "encode",
        [enc_slot_t, enc_mask_t, x_far, w_embed, enc_send, proj, recv, enc_out, latent, proc_send, halo],
        [patch, edge_rows, edge_rows, patch, patch, patch_f32, ((m, 128), F32), ((edges_e, width), BF), far_rows,
         far_rows],
        [((near + far, width), BF), ((edges_e, near + far), BF), ((edges_e, width), F32)],
        place=True,
    )

    from_one, from_two = swapped(to_one, 1), swapped(to_two, 0)

    after = (x_t, lat, slope_near, proc_recv, proc_out, cotangent, proc_slot_t, proc_mask_t, mid)
    x_t, lat, slope_near, proc_recv, proc_out, cotangent, proc_slot_t, proc_mask_t, mid = lax.optimization_barrier(after)
    x_t, lat, slope_near, proc_recv, proc_out, cotangent, proc_slot_t, proc_mask_t = call(
        load_body,
        "load",
        [Kept(v) for v in (x_t, lat, slope_near, proc_recv, proc_out, cotangent, proc_slot_t, proc_mask_t)],
        [],
        weight=FIRST[3],
    )

    wide = m + 2 * depth
    out, back_one, back_two, grad_rows, grad_mid, agg2, grad_u, grad_recv = call(
        process_body,
        "process",
        [proc_slot_t, proc_mask_t, mesh_proj, from_one, from_two, mid, proc_recv, proc_out, cotangent],
        [(*patch, "far"), edge_rows, edge_rows, patch_f32, patch_f32, patch, patch, patch],
        [((wide, width), BF), ((edges_p, wide), BF), ((wide, edges_p), BF), ((edges_p, width), F32),
         ((edges_p, width), F32), ((edges_p, width), BF)],
        place=True,
        weight=FIRST[4],
    )

    back_one, back_two = swapped(back_one, 1), swapped(back_two, 0)

    def halves(count):
        rows = count * width // 2
        return [((rows, width), F32), ((rows, width), BF)]

    square = ((width, width), F32)

    keep, send = call(
        functools.partial(process_grads_body, ORDER_P), "process_grads", [agg2, grad_u, mid, grad_recv], halves(2),
        [square] * 2, True, None, FIRST[5],
    )
    sums = {"p": Sum("process", ORDER_P, rest, keep, send, [square] * 2)}
    token = keep
    for item, weight in PLAN:
        if item == "mesh":
            keep, send, grad_msg = call(
                functools.partial(mesh_grads_body, ORDER_M),
                "mesh_grads",
                [back_one, back_two, halo, grad_rows, proc_send, grad_mid, y, r, enc_out, slope, mid,
                 agg, latent],
                halves(3) + [((edges_e, width), BF)],
                [square] * 3,
                True,
                token,
                weight,
            )
            token = keep
            sums["m"] = Sum("mesh", ORDER_M, rest, keep, send, [square] * 3)
        elif item == "grid":
            keep, send = call(
                functools.partial(grid_grads_body, ORDER_G),
                "grid_grads",
                [enc_slot_t, grad_msg, enc_send, slope_near, slope_far, x_t, x_far, lat, lat_far],
                halves(2),
                [((near + far, edges_e), BF)] + [square] * 2,
                True,
                token,
                weight,
            )
            token = keep
            sums["g"] = Sum("grid", ORDER_G, rest, keep, send, [square, ((fin, width), F32)], [square])
        else:
            token = sums[item].step(token, weight)
    for total in sums.values():
        while total.results is None:
            token = total.step(token, 0)
    g_pout, g_precv = sums["p"].results
    g_psend, g_eout, g_erecv = sums["m"].results
    g_esend, g_embed = sums["g"].results
    return out, g_embed, g_esend, g_erecv, g_eout, g_psend, g_precv, g_pout


def solution(mesh):
    rows = P(("groups", "space"), None)
    lists = P(("groups", "space"), None, None)
    return jax.shard_map(
        local,
        mesh=mesh,
        in_specs=(rows, rows, rows, lists, rows, rows, lists, rows, rows) + (P(),) * 7,
        out_specs=(rows,) + (P("groups", None),) * 7,
        check_vma=False,
    )
```

```python
import functools

import jax
import jax.numpy as jnp
from jax import lax
from jax.experimental import pallas as pl
from jax.experimental.pallas import tpu as pltpu
from jax.sharding import PartitionSpec as P

BF = jnp.bfloat16
F32 = jnp.float32
VMEM_BYTES = 16 * 1024 * 1024
BLOCKS = 8
ORDER_P, ORDER_M, ORDER_G = (1, 2, 4), (1, 2, 4), (1, 4, 2)
PLAN = (("p", 3), ("mesh", 3), ("grid", 3), ("m", 3), ("p", 3), ("g", 3), ("p", 2), ("m", 3), ("g", 2), ("m", 3), ("p", 2), ("g", 3), ("p", 3), ("m", 3), ("g", 3), ("p", 3), ("m", 3), ("g", 3), ("p", 3), ("g", 3), ("m", 3), ("g", 4), ("m", 3))
WEIGHTS = (1, 10**9, 3 * 10**9, 10**10, 3 * 10**10, 10**11)
FIRST = (0, 0, 0, 0, 0, 0)


def dot(a, b):
    return lax.dot_general(a, b, (((1,), (0,)), ((), ())), preferred_element_type=F32)


def dot_t(a, b):
    return lax.dot_general(a, b, (((1,), (1,)), ((), ())), preferred_element_type=F32)


def t_dot(a, b):
    return lax.dot_general(a, b, (((0,), (0,)), ((), ())), preferred_element_type=F32)


def sigmoid(v):
    return 0.5 * jnp.tanh(0.5 * v) + 0.5


def silu_slope(v, s):
    return s * (1.0 + v * (1.0 - s))


def normalized(u):
    c = u - jnp.mean(u, axis=-1, keepdims=True)
    r = lax.rsqrt(jnp.mean(c * c, axis=-1, keepdims=True) + 1e-05)
    return c * r, r


def normalized_grad(y, r, g):
    return r * (g - jnp.mean(g, axis=-1, keepdims=True) - y * jnp.mean(g * y, axis=-1, keepdims=True))


class Far:
    def __init__(self, value):
        self.value = pltpu.with_memory_space_constraint(value, pltpu.HBM)
        self.shape, self.dtype = value.shape, value.dtype


class Kept:
    def __init__(self, value):
        self.value = pltpu.with_memory_space_constraint(value, pltpu.HBM)
        self.shape, self.dtype = value.shape, value.dtype


class Input:
    def __init__(self, source, held=None, sem=None):
        self.held, self.copy = source if held is None else held, None
        if held is not None:
            self.copy = pltpu.make_async_copy(source, held, sem)
            self.copy.start()

    def __call__(self):
        if self.copy is not None:
            self.copy.wait()
            self.copy = None
        return self.held


class Output:
    def __init__(self, target, held=None, sem=None):
        self.held, self.copy, self.started = target if held is None else held, None, False
        if held is not None:
            self.copy = pltpu.make_async_copy(held, target, sem)

    def send(self):
        if self.copy is not None:
            self.copy.start()
        self.started = True

    def set(self, value):
        self.held[...] = value.astype(self.held.dtype)
        self.send()


def call(body, name, ins, outs, scratch=(), place=False, after=None, weight=0):
    kept = [v for v in ins if isinstance(v, Kept)]
    far_in = [isinstance(v, (Far, Kept)) for v in ins]
    far_out = [len(v) > 2 for v in outs]
    n_in, n_out, n_kept = len(ins), len(outs), len(kept)
    lead = () if after is None else (after,)

    def kernel(*refs):
        refs = refs[len(lead) :]
        sources, targets = refs[:n_in], refs[n_in : n_in + n_out]
        kept_refs = list(refs[n_in + n_out : n_in + n_out + n_kept])
        rest = list(refs[n_in + n_out + n_kept :])
        out_sems, in_sems = rest.pop(), rest.pop()
        inputs, outputs = [], []
        for i, v in enumerate(ins):
            if isinstance(v, Kept):
                inputs.append(Input(sources[i], kept_refs.pop(0), in_sems.at[i]))
            elif isinstance(v, Far):
                inputs.append(Input(sources[i], rest.pop(0), in_sems.at[i]))
            else:
                inputs.append(Input(sources[i]))
        for i, is_far in enumerate(far_out):
            outputs.append(Output(targets[i], rest.pop(0), out_sems.at[i]) if is_far else Output(targets[i]))
        where = (lax.axis_index("space").astype(jnp.int32),) if place else ()
        body(*where, inputs, outputs, rest)
        for value in inputs:
            value()
        for value in outputs:
            if not value.started:
                value.send()
        for value in outputs:
            if value.copy is not None:
                value.copy.wait()

    anywhere, near = pl.BlockSpec(memory_space=pl.ANY), pl.BlockSpec(memory_space=pltpu.VMEM)
    held = [pltpu.VMEM(v.shape, v.dtype) for v in ins if isinstance(v, Far)]
    held += [pltpu.VMEM(v[0], v[1]) for v in outs if len(v) > 2]
    return pl.pallas_call(
        kernel,
        name=name,
        out_shape=[(pltpu.HBM if far else pltpu.VMEM)(v[0], v[1]) for v, far in zip(outs, far_out)]
        + [pltpu.VMEM(v.shape, v.dtype) for v in kept],
        in_specs=[anywhere] * len(lead) + [anywhere if far else near for far in far_in],
        out_specs=[anywhere if far else near for far in far_out] + [near] * n_kept,
        scratch_shapes=held
        + [pltpu.VMEM(shape, dtype) for shape, dtype in scratch]
        + [pltpu.SemaphoreType.DMA((n_in,)), pltpu.SemaphoreType.DMA((max(n_out, 1),))],
        compiler_params=pltpu.CompilerParams(vmem_limit_bytes=VMEM_BYTES),
        cost_estimate=pl.CostEstimate(flops=WEIGHTS[weight], bytes_accessed=1, transcendentals=0),
    )(*lead, *(v.value if far else v for v, far in zip(ins, far_in)))


def pick_body(ins, outs, _):
    sends_t, x_t = ins
    sends = sends_t()[...]
    cap, peers = sends.shape
    lanes = lax.broadcasted_iota(jnp.int32, (cap, x_t.held.shape[1]), 1)
    pick = [jnp.where(sends[:, d : d + 1] == lanes, 1.0, 0.0) for d in range(peers)]
    pick = jnp.concatenate(pick, axis=0).astype(BF)
    outs[0].set(dot_t(pick, x_t()[...]))


def embed_rows(pre, ws):
    s = sigmoid(pre)
    lat = (pre * s).astype(BF)
    return lat, silu_slope(pre, s).astype(BF), dot(lat, ws).astype(BF)


def embed_body(ins, outs, scratch):
    slots_t, x_t, we, ws, latent, wrecv = ins[:6]
    lat, slope, rows, recv = outs
    (onehot,) = scratch
    fill_onehot(onehot, slots_t()[...].T)
    x_t()
    at = t_dot(x_t()[...], we()[...])
    one, two, three = embed_rows(at, ws()[...])
    lat.set(one)
    slope.set(two)
    rows.set(dot(onehot[...], three))
    recv.set(dot(latent()[...], wrecv()[...]))


def fill_onehot(onehot, slots):
    m, fan = slots.shape
    wide = onehot.shape[1]
    lanes = lax.broadcasted_iota(jnp.int32, (m, wide), 1)
    for f in range(fan):
        onehot[f * m : (f + 1) * m, :] = jnp.where(slots[:, f : f + 1] == lanes, 1.0, 0.0).astype(BF)


def fill_onehot_t(onehot, slots_t):
    fan, m = slots_t.shape
    tall = onehot.shape[0]
    subs = lax.broadcasted_iota(jnp.int32, (tall, 2 * m), 0)
    for f in range(0, fan, 2):
        pair = jnp.concatenate([slots_t[f : f + 1, :], slots_t[f + 1 : f + 2, :]], axis=1)
        onehot[:, f * m : (f + 2) * m] = jnp.where(pair == subs, 1.0, 0.0).astype(BF)


def messages(rows, recv, mask, slope):
    m, fan = mask.shape
    total = None
    for f in range(fan):
        at = slice(f * m, (f + 1) * m)
        v = rows[at, :] + recv
        s = sigmoid(v)
        k = mask[:, f : f + 1].astype(F32)
        slope[at, :] = (silu_slope(v, s) * k).astype(slope.dtype)
        part = v * s * k
        total = part if total is None else total + part
    return total.astype(BF)


def encode_body(near, me, ins, outs, scratch):
    slots_t, mask_t, x, we, ws, rows_near, recv, wout, latent, wnext, halo = ins
    mid, one, two, mesh_proj, agg, y, r, slope, lat_far, slope_far = outs
    onehot, rows = scratch
    fill_onehot(onehot, slots_t()[...].T - near)
    mask = mask_t()[...].T
    x()
    pre = dot(x()[...], we()[...])
    lat, bend, far = embed_rows(pre, ws()[...])
    lat_far.set(lat)
    slope_far.set(bend)
    rows[...] = rows_near()[...].astype(F32) + dot(onehot[...], far)
    summed = messages(rows, recv()[...], mask, slope.held)
    slope.send()
    agg.set(summed)
    normed, scale = normalized(dot(summed, wout()[...]))
    y.set(normed)
    r.set(jnp.broadcast_to(scale, r.held.shape))
    middle = (latent()[...].astype(F32) + normed).astype(BF)
    mid.set(middle)
    sent = dot(middle, wnext()[...]).astype(BF)
    mesh_proj.set(sent)
    lists = halo()[...]
    subs = lax.broadcasted_iota(jnp.int32, (sent.shape[0], lists.shape[1]), 0)
    odd = 1 - me % 2
    for out, towards in ((one, 1 - odd), (two, odd)):
        rows = jnp.where(towards == 0, lists[0:1, :], lists[1:2, :])
        out.set(t_dot(jnp.where(rows == subs, 1.0, 0.0).astype(BF), sent))


def process_body(me, ins, outs, scratch):
    onehot, onehot_t, recv, mask_t, mesh_proj, one, two, mid, wrecv, wout, cotangent = ins
    out, back_one, back_two, grad_rows, grad_mid, agg, grad_u, grad_recv = outs
    table, rows, slope, grad_msg = scratch
    m = mesh_proj.held.shape[0]
    depth = one.held.shape[0]
    odd = me % 2 == 0
    mask = mask_t()[...].T
    table[:m, :] = mesh_proj()[...]
    from_one, from_two = one()[...], two()[...]
    table[m : m + depth, :] = jnp.where(odd, from_one, from_two)
    table[m + depth : m + 2 * depth, :] = jnp.where(odd, from_two, from_one)
    rows[...] = dot(onehot()[...], table[...])
    middle = mid()[...]
    summed = messages(rows, recv()[...], mask, slope)
    agg.set(summed)
    normed, scale = normalized(dot(summed, wout()[...]))
    out.set(middle.astype(F32) + normed)
    ct = cotangent()[...].astype(F32)
    gu = normalized_grad(normed, scale, ct).astype(BF)
    grad_u.set(gu)
    gr = message_grads(grad_msg, slope, dot_t(gu, wout()[...]), mask.shape[1])
    grad_recv.set(gr)
    grads = dot(onehot_t()[...], grad_msg[...])
    to_left, to_right = grads[m : m + depth, :], grads[m + depth :, :]
    back_one.set(jnp.where(odd, to_left, to_right))
    back_two.set(jnp.where(odd, to_right, to_left))
    grad_rows.set(grads[:m, :])
    grad_mid.set(ct + dot_t(gr, wrecv()[...]))


def message_grads(grad_msg, slope, gagg, fan):
    m = gagg.shape[0]
    total = None
    for f in range(fan):
        at = slice(f * m, (f + 1) * m)
        g = slope[at, :].astype(F32) * gagg
        grad_msg[at, :] = g.astype(BF)
        total = g if total is None else total + g
    return total.astype(BF)


def block_of(place, me, order):
    flips = 0
    for i, step in enumerate(order):
        if place >> (len(order) - 1 - i) & 1:
            flips ^= step
    return (me & (BLOCKS - 1)) ^ flips


def spread(me, order, grads, keep, send):
    deep = grads[0].shape[0] // BLOCKS
    half = BLOCKS // 2
    for place in reversed(range(BLOCKS)):
        at = pl.multiple_of(block_of(place, me, order) * deep, deep)
        for g, grad in enumerate(grads):
            to = ((place % half) * len(grads) + g) * deep
            target = keep if place < half else send
            target.held[to : to + deep, :] = grad[pl.ds(at, deep), :].astype(target.held.dtype)
        if place == half:
            send.send()
    keep.send()


def process_grads_body(order, me, ins, outs, scratch):
    agg, grad_u, mid, grad_recv = ins
    one, two = scratch
    one[...] = t_dot(agg()[...], grad_u()[...])
    two[...] = t_dot(mid()[...], grad_recv()[...])
    spread(me, order, (one, two), *outs)


def mesh_grads_body(order, me, ins, outs, scratch):
    back_one, back_two, halo, grad_rows, wnext, grad_mid, y, r, wout, slope, mid, agg, latent = ins
    keep, send, grad_msg = outs
    g_next, g_out, g_recv = scratch
    m = mid.held.shape[0]
    lists = halo()[...]
    subs = lax.broadcasted_iota(jnp.int32, (m, lists.shape[1]), 0)
    odd = me % 2 == 0
    put_one = jnp.where(jnp.where(odd, lists[0:1, :], lists[1:2, :]) == subs, 1.0, 0.0).astype(BF)
    put_two = jnp.where(jnp.where(odd, lists[1:2, :], lists[0:1, :]) == subs, 1.0, 0.0).astype(BF)
    gp = (grad_rows()[...] + dot(put_one, back_one()[...]) + dot(put_two, back_two()[...])).astype(BF)
    gmid = grad_mid()[...] + dot_t(gp, wnext()[...])
    gu = normalized_grad(y()[...], r()[:, 0:1], gmid).astype(BF)
    gagg = dot_t(gu, wout()[...])
    gr = message_grads(grad_msg.held, slope(), gagg, grad_msg.held.shape[0] // m)
    g_next[...] = t_dot(mid()[...], gp)
    g_out[...] = t_dot(agg()[...], gu)
    g_recv[...] = t_dot(latent()[...], gr)
    spread(me, order, (g_next, g_out, g_recv), keep, send)


def grid_grads_body(order, me, ins, outs, scratch):
    onehot_t, grad_msg, ws, slope_near, slope_far, x_t, x_far, lat, lat_far = ins
    g_send, g_embed = scratch
    near = lat.held.shape[0]
    grad_table = dot(onehot_t()[...], grad_msg()[...]).astype(BF)
    g_near, g_far = grad_table[:near, :], grad_table[near:, :]
    p_near = (dot_t(g_near, ws()[...]) * slope_near()[...].astype(F32)).astype(BF)
    p_far = (dot_t(g_far, ws()[...]) * slope_far()[...].astype(F32)).astype(BF)
    fin = x_t.held.shape[0]
    tail = fin // 32 * 32
    g_embed[tail:, :] = jnp.zeros((g_embed.shape[0] - tail, g_embed.shape[1]), F32)
    g_embed[:fin, :] = dot(x_t()[...], p_near) + t_dot(x_far()[...], p_far)
    g_send[...] = t_dot(lat()[...], g_near) + t_dot(lat_far()[...], g_far)
    spread(me, order, (g_send, g_embed), *outs)


def collect_body(order, me, ins, outs, scratch):
    whole = scratch[0] if scratch else outs[0].held
    half = BLOCKS // 2
    deep = whole.shape[0] // BLOCKS
    for g, out in enumerate(outs):
        short = out.held.shape[0] != whole.shape[0]
        for place in range(BLOCKS):
            source = ins[place // half]()
            at = pl.multiple_of(block_of(place, me, order) * deep, deep)
            frm = ((place % half) * len(outs) + g) * deep
            (whole if short else out.held)[pl.ds(at, deep), :] = source[frm : frm + deep, :].astype(F32)
        if short:
            out.held[...] = whole[: out.held.shape[0], :]
        out.send()


def add_body(ins, outs, _):
    kept, got = ins
    total = kept()[...].astype(F32) + got()[...].astype(F32)
    deep = 0
    for out in outs:
        out.set(total[deep : deep + out.held.shape[0], :])
        deep += out.held.shape[0]


def join_body(ins, outs, _):
    half = ins[0].held.shape[0]
    outs[0].held[:half, :] = ins[0]()[...]
    outs[0].held[half:, :] = ins[1]()[...]


def load_body(ins, outs, _):
    slots_t, mid, wrecv, enc_slots_t = ins[:4]
    onehot, onehot_t, enc_onehot_t, recv = outs
    slots = slots_t()[...]
    fill_onehot(onehot.held, slots.T)
    fill_onehot_t(onehot_t.held, slots)
    fill_onehot_t(enc_onehot_t.held, enc_slots_t()[...])
    recv.set(dot(mid()[...], wrecv()[...]))


def exchange(value, step):
    n = lax.axis_size("space")
    return lax.ppermute(value, "space", [(i, i ^ step) for i in range(n)])


class Sum:
    def __init__(self, name, order, rest, keep, send, outs, scratch=()):
        self.name, self.order, self.outs, self.scratch = name, order, [(*v, "far") for v in outs], scratch
        halve = [("halve", order[i + 1]) for i in range(len(order) - 1)]
        whole = [("add", step) for step in (*rest, order[-1])]
        double = [("join", step) for step in order[-2::-1]]
        self.steps = halve + whole + double
        self.value, self.results = keep, None
        self.coming = exchange(send, order[0])

    def step(self, after, weight):
        rows, width = self.value.shape
        ins = [self.value, self.coming]
        if not self.steps:
            body = functools.partial(collect_body, self.order)
            self.results = call(body, f"{self.name}_collect", ins, self.outs, self.scratch, True, after, weight)
            return pltpu.with_memory_space_constraint(self.results[0], pltpu.HBM)
        kind, step = self.steps.pop(0)
        if kind == "halve":
            made = [((rows // 2, width), F32), ((rows // 2, width), BF)]
            self.value, sent = call(add_body, f"{self.name}_add", ins, made, after=after, weight=weight)
        else:
            body, made = (add_body, rows) if kind == "add" else (join_body, 2 * rows)
            (self.value,) = call(body, f"{self.name}_{kind}", ins, [((made, width), BF)], after=after, weight=weight)
            sent = self.value
        self.coming = exchange(sent, step)
        return self.value


def swapped(rows, first):
    n = lax.axis_size("space")
    pairs = [((first + i) % n, (first + i + 1) % n) for i in range(0, n, 2)]
    return lax.ppermute(rows, "space", [*pairs, *((b, a) for a, b in pairs)])


def local(
    grid_inputs, mesh_latent, cotangent, send_list, enc_slot, enc_mask, halo_list, proc_slot, proc_mask,
    w_embed, enc_send, enc_recv, enc_out, proc_send, proc_recv, proc_out,
):
    n = lax.axis_size("space")
    rest = tuple(1 << i for i in range(3, n.bit_length() - 1))
    near, fin = grid_inputs.shape
    m, width = mesh_latent.shape
    edges_e = m * enc_slot.shape[1]
    edges_p = m * proc_slot.shape[1]
    depth = halo_list.shape[2]
    far = send_list.shape[1] * send_list.shape[2]
    x_t, sends_t, enc_slot_t, enc_mask_t, proc_slot_t, proc_mask_t = (
        v.T for v in (grid_inputs, send_list[0], enc_slot, enc_mask, proc_slot, proc_mask)
    )
    halo = halo_list[0]

    (outgoing,) = call(
        pick_body, "pick", [Far(sends_t), Far(x_t)], [((far, fin), BF)], weight=FIRST[0]
    )
    incoming = lax.all_to_all(outgoing.reshape(n, -1, fin), "space", split_axis=0, concat_axis=0, tiled=True)
    x_far = incoming.reshape(far, fin)

    patch, edge_rows, patch_f32 = ((m, width), BF), ((depth, width), BF), ((m, width), F32)
    grid_rows, far_rows = ((near, width), BF), ((far, width), BF)
    lat, slope_near, rows_near, recv, enc_slot_t, w_embed, enc_send, latent, enc_out, proc_send, halo, enc_mask_t = call(
        embed_body,
        "embed",
        [Kept(enc_slot_t), Far(x_t), Kept(w_embed), Kept(enc_send), Kept(mesh_latent), Far(enc_recv), Kept(enc_out),
         Kept(proc_send), Kept(halo), Kept(enc_mask_t)],
        [(*grid_rows, "far"), (*grid_rows, "far"), ((edges_e, width), BF), patch_f32],
        [((edges_e, near), BF)],
        weight=FIRST[1],
    )

    mid, to_one, to_two, mesh_proj, agg, y, r, slope, lat_far, slope_far = call(
        functools.partial(encode_body, near),
        "encode",
        [enc_slot_t, enc_mask_t, x_far, w_embed, enc_send, rows_near, recv, enc_out, latent, proc_send, halo],
        [patch, edge_rows, edge_rows, patch, patch, patch_f32, ((m, 128), F32), ((edges_e, width), BF), far_rows,
         far_rows],
        [((edges_e, far), BF), ((edges_e, width), F32)],
        place=True,
    )

    from_one, from_two = swapped(to_one, 1), swapped(to_two, 0)

    wide = m + 2 * depth
    later = (proc_slot_t, proc_recv, x_t, lat, slope_near, proc_out, cotangent, proc_mask_t)
    *later, mid = lax.optimization_barrier((*later, mid))
    onehot_p, onehot_p_t, onehot_e_t, recv_p, proc_recv, x_t, lat, slope_near, proc_out, cotangent, proc_mask_t = call(
        load_body,
        "load",
        [Far(later[0]), mid, Kept(later[1]), enc_slot_t, *(Kept(v) for v in later[2:])],
        [((edges_p, wide), BF), ((wide, edges_p), BF), ((near + far, edges_e), BF), patch_f32],
        weight=FIRST[3],
    )

    out, back_one, back_two, grad_rows, grad_mid, agg2, grad_u, grad_recv = call(
        process_body,
        "process",
        [onehot_p, onehot_p_t, recv_p, proc_mask_t, mesh_proj, from_one, from_two, mid, proc_recv, proc_out, cotangent],
        [(*patch, "far"), edge_rows, edge_rows, patch_f32, patch_f32, patch, patch, patch],
        [((wide, width), BF), ((edges_p, width), F32), ((edges_p, width), F32), ((edges_p, width), BF)],
        place=True,
        weight=FIRST[4],
    )

    back_one, back_two = swapped(back_one, 1), swapped(back_two, 0)

    def halves(count):
        rows = count * width // 2
        return [((rows, width), F32), ((rows, width), BF)]

    square = ((width, width), F32)

    keep, send = call(
        functools.partial(process_grads_body, ORDER_P), "process_grads", [agg2, grad_u, mid, grad_recv], halves(2),
        [square] * 2, True, None, FIRST[5],
    )
    sums = {"p": Sum("process", ORDER_P, rest, keep, send, [square] * 2)}
    token = keep
    for item, weight in PLAN:
        if item == "mesh":
            keep, send, grad_msg = call(
                functools.partial(mesh_grads_body, ORDER_M),
                "mesh_grads",
                [back_one, back_two, halo, grad_rows, proc_send, grad_mid, y, r, enc_out, slope, mid,
                 agg, latent],
                halves(3) + [((edges_e, width), BF)],
                [square] * 3,
                True,
                token,
                weight,
            )
            token = keep
            sums["m"] = Sum("mesh", ORDER_M, rest, keep, send, [square] * 3)
        elif item == "grid":
            keep, send = call(
                functools.partial(grid_grads_body, ORDER_G),
                "grid_grads",
                [onehot_e_t, grad_msg, enc_send, slope_near, slope_far, x_t, x_far, lat, lat_far],
                halves(2),
                [square] * 2,
                True,
                token,
                weight,
            )
            token = keep
            sums["g"] = Sum("grid", ORDER_G, rest, keep, send, [square, ((fin, width), F32)], [square])
        else:
            token = sums[item].step(token, weight)
    for total in sums.values():
        while total.results is None:
            token = total.step(token, 0)
    g_pout, g_precv = sums["p"].results
    g_psend, g_eout, g_erecv = sums["m"].results
    g_esend, g_embed = sums["g"].results
    return out, g_embed, g_esend, g_erecv, g_eout, g_psend, g_precv, g_pout


def solution(mesh):
    rows = P(("groups", "space"), None)
    lists = P(("groups", "space"), None, None)
    return jax.shard_map(
        local,
        mesh=mesh,
        in_specs=(rows, rows, rows, lists, rows, rows, lists, rows, rows) + (P(),) * 7,
        out_specs=(rows,) + (P("groups", None),) * 7,
        check_vma=False,
    )
```

```python
import functools

import jax
import jax.numpy as jnp
from jax import lax
from jax.experimental import pallas as pl
from jax.experimental.pallas import tpu as pltpu
from jax.sharding import PartitionSpec as P

BF = jnp.bfloat16
F32 = jnp.float32
VMEM_BYTES = 16 * 1024 * 1024
BLOCKS = 8
ORDER_P, ORDER_M, ORDER_G = (1, 2, 4), (1, 2, 4), (1, 4, 2)
PLAN = (("p", 3), ("mesh", 3), ("grid", 3), ("m", 3), ("p", 3), ("g", 3), ("p", 2), ("m", 3), ("g", 2), ("m", 3), ("p", 2), ("g", 3), ("p", 3), ("m", 3), ("g", 3), ("p", 3), ("m", 3), ("g", 3), ("p", 3), ("g", 3), ("m", 3), ("g", 4), ("m", 3))
WEIGHTS = (1, 10**9, 3 * 10**9, 10**10, 3 * 10**10, 10**11)
FIRST = (0, 0, 0, 0, 0, 0)


def dot(a, b):
    return lax.dot_general(a, b, (((1,), (0,)), ((), ())), preferred_element_type=F32)


def dot_t(a, b):
    return lax.dot_general(a, b, (((1,), (1,)), ((), ())), preferred_element_type=F32)


def t_dot(a, b):
    return lax.dot_general(a, b, (((0,), (0,)), ((), ())), preferred_element_type=F32)


def sigmoid(v):
    return 0.5 * jnp.tanh(0.5 * v) + 0.5


def silu_slope(v, s):
    return s * (1.0 + v * (1.0 - s))


def normalized(u):
    c = u - jnp.mean(u, axis=-1, keepdims=True)
    r = lax.rsqrt(jnp.mean(c * c, axis=-1, keepdims=True) + 1e-05)
    return c * r, r


def normalized_grad(y, r, g):
    return r * (g - jnp.mean(g, axis=-1, keepdims=True) - y * jnp.mean(g * y, axis=-1, keepdims=True))


class Far:
    def __init__(self, value):
        self.value = pltpu.with_memory_space_constraint(value, pltpu.HBM)
        self.shape, self.dtype = value.shape, value.dtype


class Kept:
    def __init__(self, value):
        self.value = pltpu.with_memory_space_constraint(value, pltpu.HBM)
        self.shape, self.dtype = value.shape, value.dtype


class Input:
    def __init__(self, source, held=None, sem=None):
        self.held, self.copy = source if held is None else held, None
        if held is not None:
            self.copy = pltpu.make_async_copy(source, held, sem)
            self.copy.start()

    def __call__(self):
        if self.copy is not None:
            self.copy.wait()
            self.copy = None
        return self.held


class Output:
    def __init__(self, target, held=None, sem=None):
        self.held, self.copy, self.started = target if held is None else held, None, False
        if held is not None:
            self.copy = pltpu.make_async_copy(held, target, sem)

    def send(self):
        if self.copy is not None:
            self.copy.start()
        self.started = True

    def set(self, value):
        self.held[...] = value.astype(self.held.dtype)
        self.send()


def call(body, name, ins, outs, scratch=(), place=False, after=None, weight=0):
    kept = [v for v in ins if isinstance(v, Kept)]
    far_in = [isinstance(v, (Far, Kept)) for v in ins]
    far_out = [len(v) > 2 for v in outs]
    n_in, n_out, n_kept = len(ins), len(outs), len(kept)
    lead = () if after is None else (after,)

    def kernel(*refs):
        refs = refs[len(lead) :]
        sources, targets = refs[:n_in], refs[n_in : n_in + n_out]
        kept_refs = list(refs[n_in + n_out : n_in + n_out + n_kept])
        rest = list(refs[n_in + n_out + n_kept :])
        out_sems, in_sems = rest.pop(), rest.pop()
        inputs, outputs = [], []
        for i, v in enumerate(ins):
            if isinstance(v, Kept):
                inputs.append(Input(sources[i], kept_refs.pop(0), in_sems.at[i]))
            elif isinstance(v, Far):
                inputs.append(Input(sources[i], rest.pop(0), in_sems.at[i]))
            else:
                inputs.append(Input(sources[i]))
        for i, is_far in enumerate(far_out):
            outputs.append(Output(targets[i], rest.pop(0), out_sems.at[i]) if is_far else Output(targets[i]))
        where = (lax.axis_index("space").astype(jnp.int32),) if place else ()
        body(*where, inputs, outputs, rest)
        for value in inputs:
            value()
        for value in outputs:
            if not value.started:
                value.send()
        for value in outputs:
            if value.copy is not None:
                value.copy.wait()

    anywhere, near = pl.BlockSpec(memory_space=pl.ANY), pl.BlockSpec(memory_space=pltpu.VMEM)
    held = [pltpu.VMEM(v.shape, v.dtype) for v in ins if isinstance(v, Far)]
    held += [pltpu.VMEM(v[0], v[1]) for v in outs if len(v) > 2]
    return pl.pallas_call(
        kernel,
        name=name,
        out_shape=[(pltpu.HBM if far else pltpu.VMEM)(v[0], v[1]) for v, far in zip(outs, far_out)]
        + [pltpu.VMEM(v.shape, v.dtype) for v in kept],
        in_specs=[anywhere] * len(lead) + [anywhere if far else near for far in far_in],
        out_specs=[anywhere if far else near for far in far_out] + [near] * n_kept,
        scratch_shapes=held
        + [pltpu.VMEM(shape, dtype) for shape, dtype in scratch]
        + [pltpu.SemaphoreType.DMA((n_in,)), pltpu.SemaphoreType.DMA((max(n_out, 1),))],
        compiler_params=pltpu.CompilerParams(vmem_limit_bytes=VMEM_BYTES),
        cost_estimate=pl.CostEstimate(flops=WEIGHTS[weight], bytes_accessed=1, transcendentals=0),
    )(*lead, *(v.value if far else v for v, far in zip(ins, far_in)))


def pick_body(ins, outs, _):
    sends_t, x_t = ins
    sends = sends_t()[...]
    cap, peers = sends.shape
    lanes = lax.broadcasted_iota(jnp.int32, (cap, x_t.held.shape[1]), 1)
    pick = [jnp.where(sends[:, d : d + 1] == lanes, 1.0, 0.0) for d in range(peers)]
    pick = jnp.concatenate(pick, axis=0).astype(BF)
    outs[0].set(dot_t(pick, x_t()[...]))


def embed_rows(pre, ws):
    s = sigmoid(pre)
    lat = (pre * s).astype(BF)
    return lat, silu_slope(pre, s).astype(BF), dot(lat, ws).astype(BF)


def embed_body(ins, outs, scratch):
    slots_t, x_t, we, ws, latent, wrecv = ins[:6]
    lat, slope, rows, recv = outs
    (onehot,) = scratch
    fill_onehot(onehot, slots_t()[...].T)
    x_t()
    at = t_dot(x_t()[...], we()[...])
    one, two, three = embed_rows(at, ws()[...])
    lat.set(one)
    slope.set(two)
    rows.set(dot(onehot[...], three))
    recv.set(0.5 * dot(latent()[...], wrecv()[...]))


def fill_onehot(onehot, slots):
    m, fan = slots.shape
    wide = onehot.shape[1]
    lanes = lax.broadcasted_iota(jnp.int32, (m, wide), 1)
    for f in range(fan):
        onehot[f * m : (f + 1) * m, :] = jnp.where(slots[:, f : f + 1] == lanes, 0.5, 0.0).astype(BF)


def fill_onehot_t(onehot, slots_t):
    fan, m = slots_t.shape
    tall = onehot.shape[0]
    subs = lax.broadcasted_iota(jnp.int32, (tall, 2 * m), 0)
    for f in range(0, fan, 2):
        pair = jnp.concatenate([slots_t[f : f + 1, :], slots_t[f + 1 : f + 2, :]], axis=1)
        onehot[:, f * m : (f + 2) * m] = jnp.where(pair == subs, 1.0, 0.0).astype(BF)


def messages(rows, recv, mask, slope):
    m, fan = mask.shape
    total = None
    for f in range(fan):
        at = slice(f * m, (f + 1) * m)
        h = rows[at, :] + recv
        t = jnp.tanh(h)
        q = 1.0 + t
        p = h * q
        k = mask[:, f : f + 1].astype(F32)
        slope[at, :] = ((q + p * (1.0 - t)) * (0.5 * k)).astype(slope.dtype)
        part = p * k
        total = part if total is None else total + part
    return total.astype(BF)


def encode_body(near, me, ins, outs, scratch):
    slots_t, mask_t, x, we, ws, rows_near, recv, wout, latent, wnext, halo = ins
    mid, one, two, mesh_proj, agg, y, r, slope, lat_far, slope_far = outs
    onehot, rows = scratch
    fill_onehot(onehot, slots_t()[...].T - near)
    mask = mask_t()[...].T
    x()
    pre = dot(x()[...], we()[...])
    lat, bend, far = embed_rows(pre, ws()[...])
    lat_far.set(lat)
    slope_far.set(bend)
    rows[...] = rows_near()[...].astype(F32) + dot(onehot[...], far)
    summed = messages(rows, recv()[...], mask, slope.held)
    slope.send()
    agg.set(summed)
    normed, scale = normalized(dot(summed, wout()[...]))
    y.set(normed)
    r.set(jnp.broadcast_to(scale, r.held.shape))
    middle = (latent()[...].astype(F32) + normed).astype(BF)
    mid.set(middle)
    sent = dot(middle, wnext()[...]).astype(BF)
    mesh_proj.set(sent)
    lists = halo()[...]
    subs = lax.broadcasted_iota(jnp.int32, (sent.shape[0], lists.shape[1]), 0)
    odd = 1 - me % 2
    for out, towards in ((one, 1 - odd), (two, odd)):
        rows = jnp.where(towards == 0, lists[0:1, :], lists[1:2, :])
        out.set(t_dot(jnp.where(rows == subs, 1.0, 0.0).astype(BF), sent))


def process_body(me, ins, outs, scratch):
    onehot, onehot_t, recv, mask_t, mesh_proj, one, two, mid, wrecv, wout, cotangent = ins
    out, back_one, back_two, grad_rows, grad_mid, agg, grad_u, grad_recv = outs
    table, rows, slope, grad_msg = scratch
    m = mesh_proj.held.shape[0]
    depth = one.held.shape[0]
    odd = me % 2 == 0
    mask = mask_t()[...].T
    table[:m, :] = mesh_proj()[...]
    from_one, from_two = one()[...], two()[...]
    table[m : m + depth, :] = jnp.where(odd, from_one, from_two)
    table[m + depth : m + 2 * depth, :] = jnp.where(odd, from_two, from_one)
    rows[...] = dot(onehot()[...], table[...])
    middle = mid()[...]
    summed = messages(rows, recv()[...], mask, slope)
    agg.set(summed)
    normed, scale = normalized(dot(summed, wout()[...]))
    out.set(middle.astype(F32) + normed)
    ct = cotangent()[...].astype(F32)
    gu = normalized_grad(normed, scale, ct).astype(BF)
    grad_u.set(gu)
    gr = message_grads(grad_msg, slope, dot_t(gu, wout()[...]), mask.shape[1])
    grad_recv.set(gr)
    grads = dot(onehot_t()[...], grad_msg[...])
    to_left, to_right = grads[m : m + depth, :], grads[m + depth :, :]
    back_one.set(jnp.where(odd, to_left, to_right))
    back_two.set(jnp.where(odd, to_right, to_left))
    grad_rows.set(grads[:m, :])
    grad_mid.set(ct + dot_t(gr, wrecv()[...]))


def message_grads(grad_msg, slope, gagg, fan):
    m = gagg.shape[0]
    total = None
    for f in range(fan):
        at = slice(f * m, (f + 1) * m)
        g = slope[at, :].astype(F32) * gagg
        grad_msg[at, :] = g.astype(BF)
        total = g if total is None else total + g
    return total.astype(BF)


def block_of(place, me, order):
    flips = 0
    for i, step in enumerate(order):
        if place >> (len(order) - 1 - i) & 1:
            flips ^= step
    return (me & (BLOCKS - 1)) ^ flips


def spread(me, order, grads, keep, send):
    deep = grads[0].shape[0] // BLOCKS
    half = BLOCKS // 2
    for place in reversed(range(BLOCKS)):
        at = pl.multiple_of(block_of(place, me, order) * deep, deep)
        for g, grad in enumerate(grads):
            to = ((place % half) * len(grads) + g) * deep
            target = keep if place < half else send
            target.held[to : to + deep, :] = grad[pl.ds(at, deep), :].astype(target.held.dtype)
        if place == half:
            send.send()
    keep.send()


def process_grads_body(order, me, ins, outs, scratch):
    agg, grad_u, mid, grad_recv = ins
    one, two = scratch
    one[...] = t_dot(agg()[...], grad_u()[...])
    two[...] = t_dot(mid()[...], grad_recv()[...])
    spread(me, order, (one, two), *outs)


def mesh_grads_body(order, me, ins, outs, scratch):
    back_one, back_two, halo, grad_rows, wnext, grad_mid, y, r, wout, slope, mid, agg, latent = ins
    keep, send, grad_msg = outs
    g_next, g_out, g_recv = scratch
    m = mid.held.shape[0]
    lists = halo()[...]
    subs = lax.broadcasted_iota(jnp.int32, (m, lists.shape[1]), 0)
    odd = me % 2 == 0
    put_one = jnp.where(jnp.where(odd, lists[0:1, :], lists[1:2, :]) == subs, 1.0, 0.0).astype(BF)
    put_two = jnp.where(jnp.where(odd, lists[1:2, :], lists[0:1, :]) == subs, 1.0, 0.0).astype(BF)
    gp = (grad_rows()[...] + dot(put_one, back_one()[...]) + dot(put_two, back_two()[...])).astype(BF)
    gmid = grad_mid()[...] + dot_t(gp, wnext()[...])
    gu = normalized_grad(y()[...], r()[:, 0:1], gmid).astype(BF)
    gagg = dot_t(gu, wout()[...])
    gr = message_grads(grad_msg.held, slope(), gagg, grad_msg.held.shape[0] // m)
    g_next[...] = t_dot(mid()[...], gp)
    g_out[...] = t_dot(agg()[...], gu)
    g_recv[...] = t_dot(latent()[...], gr)
    spread(me, order, (g_next, g_out, g_recv), keep, send)


def grid_grads_body(order, me, ins, outs, scratch):
    onehot_t, grad_msg, ws, slope_near, slope_far, x_t, x_far, lat, lat_far = ins
    g_send, g_embed = scratch
    near = lat.held.shape[0]
    grad_table = dot(onehot_t()[...], grad_msg()[...]).astype(BF)
    g_near, g_far = grad_table[:near, :], grad_table[near:, :]
    p_near = (dot_t(g_near, ws()[...]) * slope_near()[...].astype(F32)).astype(BF)
    p_far = (dot_t(g_far, ws()[...]) * slope_far()[...].astype(F32)).astype(BF)
    fin = x_t.held.shape[0]
    tail = fin // 32 * 32
    g_embed[tail:, :] = jnp.zeros((g_embed.shape[0] - tail, g_embed.shape[1]), F32)
    g_embed[:fin, :] = dot(x_t()[...], p_near) + t_dot(x_far()[...], p_far)
    g_send[...] = t_dot(lat()[...], g_near) + t_dot(lat_far()[...], g_far)
    spread(me, order, (g_send, g_embed), *outs)


def collect_body(order, me, ins, outs, scratch):
    whole = scratch[0] if scratch else outs[0].held
    half = BLOCKS // 2
    deep = whole.shape[0] // BLOCKS
    for g, out in enumerate(outs):
        short = out.held.shape[0] != whole.shape[0]
        for place in range(BLOCKS):
            source = ins[place // half]()
            at = pl.multiple_of(block_of(place, me, order) * deep, deep)
            frm = ((place % half) * len(outs) + g) * deep
            (whole if short else out.held)[pl.ds(at, deep), :] = source[frm : frm + deep, :].astype(F32)
        if short:
            out.held[...] = whole[: out.held.shape[0], :]
        out.send()


def add_body(ins, outs, _):
    kept, got = ins
    total = kept()[...].astype(F32) + got()[...].astype(F32)
    deep = 0
    for out in outs:
        out.set(total[deep : deep + out.held.shape[0], :])
        deep += out.held.shape[0]


def join_body(ins, outs, _):
    half = ins[0].held.shape[0]
    outs[0].held[:half, :] = ins[0]()[...]
    outs[0].held[half:, :] = ins[1]()[...]


def load_body(ins, outs, _):
    slots_t, mid, wrecv, enc_slots_t = ins[:4]
    onehot, onehot_t, enc_onehot_t, recv = outs
    slots = slots_t()[...]
    fill_onehot(onehot.held, slots.T)
    fill_onehot_t(onehot_t.held, slots)
    fill_onehot_t(enc_onehot_t.held, enc_slots_t()[...])
    recv.set(0.5 * dot(mid()[...], wrecv()[...]))


def exchange(value, step):
    n = lax.axis_size("space")
    return lax.ppermute(value, "space", [(i, i ^ step) for i in range(n)])


class Sum:
    def __init__(self, name, order, rest, keep, send, outs, scratch=()):
        self.name, self.order, self.outs, self.scratch = name, order, [(*v, "far") for v in outs], scratch
        halve = [("halve", order[i + 1]) for i in range(len(order) - 1)]
        whole = [("add", step) for step in (*rest, order[-1])]
        double = [("join", step) for step in order[-2::-1]]
        self.steps = halve + whole + double
        self.value, self.results = keep, None
        self.coming = exchange(send, order[0])

    def step(self, after, weight):
        rows, width = self.value.shape
        ins = [self.value, self.coming]
        if not self.steps:
            body = functools.partial(collect_body, self.order)
            self.results = call(body, f"{self.name}_collect", ins, self.outs, self.scratch, True, after, weight)
            return pltpu.with_memory_space_constraint(self.results[0], pltpu.HBM)
        kind, step = self.steps.pop(0)
        if kind == "halve":
            made = [((rows // 2, width), F32), ((rows // 2, width), BF)]
            self.value, sent = call(add_body, f"{self.name}_add", ins, made, after=after, weight=weight)
        else:
            body, made = (add_body, rows) if kind == "add" else (join_body, 2 * rows)
            (self.value,) = call(body, f"{self.name}_{kind}", ins, [((made, width), BF)], after=after, weight=weight)
            sent = self.value
        self.coming = exchange(sent, step)
        return self.value


def swapped(rows, first):
    n = lax.axis_size("space")
    pairs = [((first + i) % n, (first + i + 1) % n) for i in range(0, n, 2)]
    return lax.ppermute(rows, "space", [*pairs, *((b, a) for a, b in pairs)])


def local(
    grid_inputs, mesh_latent, cotangent, send_list, enc_slot, enc_mask, halo_list, proc_slot, proc_mask,
    w_embed, enc_send, enc_recv, enc_out, proc_send, proc_recv, proc_out,
):
    n = lax.axis_size("space")
    rest = tuple(1 << i for i in range(3, n.bit_length() - 1))
    near, fin = grid_inputs.shape
    m, width = mesh_latent.shape
    edges_e = m * enc_slot.shape[1]
    edges_p = m * proc_slot.shape[1]
    depth = halo_list.shape[2]
    far = send_list.shape[1] * send_list.shape[2]
    x_t, sends_t, enc_slot_t, enc_mask_t, proc_slot_t, proc_mask_t = (
        v.T for v in (grid_inputs, send_list[0], enc_slot, enc_mask, proc_slot, proc_mask)
    )
    halo = halo_list[0]

    (outgoing,) = call(
        pick_body, "pick", [Far(sends_t), Far(x_t)], [((far, fin), BF)], weight=FIRST[0]
    )
    incoming = lax.all_to_all(outgoing.reshape(n, -1, fin), "space", split_axis=0, concat_axis=0, tiled=True)
    x_far = incoming.reshape(far, fin)

    patch, edge_rows, patch_f32 = ((m, width), BF), ((depth, width), BF), ((m, width), F32)
    grid_rows, far_rows = ((near, width), BF), ((far, width), BF)
    lat, slope_near, rows_near, recv, enc_slot_t, w_embed, enc_send, latent, enc_out, proc_send, halo, enc_mask_t = call(
        embed_body,
        "embed",
        [Kept(enc_slot_t), Far(x_t), Kept(w_embed), Kept(enc_send), Kept(mesh_latent), Far(enc_recv), Kept(enc_out),
         Kept(proc_send), Kept(halo), Kept(enc_mask_t)],
        [(*grid_rows, "far"), (*grid_rows, "far"), ((edges_e, width), BF), patch_f32],
        [((edges_e, near), BF)],
        weight=FIRST[1],
    )

    mid, to_one, to_two, mesh_proj, agg, y, r, slope, lat_far, slope_far = call(
        functools.partial(encode_body, near),
        "encode",
        [enc_slot_t, enc_mask_t, x_far, w_embed, enc_send, rows_near, recv, enc_out, latent, proc_send, halo],
        [patch, edge_rows, edge_rows, patch, patch, patch_f32, ((m, 128), F32), ((edges_e, width), BF), far_rows,
         far_rows],
        [((edges_e, far), BF), ((edges_e, width), F32)],
        place=True,
    )

    from_one, from_two = swapped(to_one, 1), swapped(to_two, 0)

    wide = m + 2 * depth
    later = (proc_slot_t, proc_recv, x_t, lat, slope_near, proc_out, cotangent, proc_mask_t)
    *later, mid = lax.optimization_barrier((*later, mid))
    onehot_p, onehot_p_t, onehot_e_t, recv_p, proc_recv, x_t, lat, slope_near, proc_out, cotangent, proc_mask_t = call(
        load_body,
        "load",
        [Far(later[0]), mid, Kept(later[1]), enc_slot_t, *(Kept(v) for v in later[2:])],
        [((edges_p, wide), BF), ((wide, edges_p), BF), ((near + far, edges_e), BF), patch_f32],
        weight=FIRST[3],
    )

    out, back_one, back_two, grad_rows, grad_mid, agg2, grad_u, grad_recv = call(
        process_body,
        "process",
        [onehot_p, onehot_p_t, recv_p, proc_mask_t, mesh_proj, from_one, from_two, mid, proc_recv, proc_out, cotangent],
        [(*patch, "far"), edge_rows, edge_rows, patch_f32, patch_f32, patch, patch, patch],
        [((wide, width), BF), ((edges_p, width), F32), ((edges_p, width), F32), ((edges_p, width), BF)],
        place=True,
        weight=FIRST[4],
    )

    back_one, back_two = swapped(back_one, 1), swapped(back_two, 0)

    def halves(count):
        rows = count * width // 2
        return [((rows, width), F32), ((rows, width), BF)]

    square = ((width, width), F32)

    keep, send = call(
        functools.partial(process_grads_body, ORDER_P), "process_grads", [agg2, grad_u, mid, grad_recv], halves(2),
        [square] * 2, True, None, FIRST[5],
    )
    sums = {"p": Sum("process", ORDER_P, rest, keep, send, [square] * 2)}
    token = keep
    for item, weight in PLAN:
        if item == "mesh":
            keep, send, grad_msg = call(
                functools.partial(mesh_grads_body, ORDER_M),
                "mesh_grads",
                [back_one, back_two, halo, grad_rows, proc_send, grad_mid, y, r, enc_out, slope, mid,
                 agg, latent],
                halves(3) + [((edges_e, width), BF)],
                [square] * 3,
                True,
                token,
                weight,
            )
            token = keep
            sums["m"] = Sum("mesh", ORDER_M, rest, keep, send, [square] * 3)
        elif item == "grid":
            keep, send = call(
                functools.partial(grid_grads_body, ORDER_G),
                "grid_grads",
                [onehot_e_t, grad_msg, enc_send, slope_near, slope_far, x_t, x_far, lat, lat_far],
                halves(2),
                [square] * 2,
                True,
                token,
                weight,
            )
            token = keep
            sums["g"] = Sum("grid", ORDER_G, rest, keep, send, [square, ((fin, width), F32)], [square])
        else:
            token = sums[item].step(token, weight)
    for total in sums.values():
        while total.results is None:
            token = total.step(token, 0)
    g_pout, g_precv = sums["p"].results
    g_psend, g_eout, g_erecv = sums["m"].results
    g_esend, g_embed = sums["g"].results
    return out, g_embed, g_esend, g_erecv, g_eout, g_psend, g_precv, g_pout


def solution(mesh):
    rows = P(("groups", "space"), None)
    lists = P(("groups", "space"), None, None)
    return jax.shard_map(
        local,
        mesh=mesh,
        in_specs=(rows, rows, rows, lists, rows, rows, lists, rows, rows) + (P(),) * 7,
        out_specs=(rows,) + (P("groups", None),) * 7,
        check_vma=False,
    )
```
